256 devices in a mesh: px: 32 (over x, y, core), py: 8 (over z).
Axes of the slice: x: 4, y: 4, z: 8, core: 2. Of those that a mesh axis runs over, the one named last changes fastest.
Arguments:
- forcing: float32 [3, 224, 56, 7, 128], P(None, 'px', 'py'), may hold values from -600 to 600
- initial_guess: float32 [3, 224, 56, 7, 128], P(None, 'px', 'py'), may hold values from -3 to 3
- forward_velocity: bfloat16 [3, 224, 56, 7, 128], P(None, 'px', 'py'), may hold values from -4 to 4
- free_mask: int32 [224, 56, 7, 128], P('px', 'py'), may hold values 0 or 1
Outputs:
- adjoint_velocity: float32 [3, 224, 56, 7, 128], P(None, 'px', 'py')
- search_direction: float32 [3, 224, 56, 7, 128], P(None, 'px', 'py')
The draws below stay inside these ranges and needn't reach their ends.
Inputs may be any that keep to these rules, and one draw needn't show every extreme that they name: `free_mask`: 1 marks a free node, 0 a node held at its initial guess.
All inputs are finite; a program needn't handle non-finite values. No bound on the sum of `free_mask` on one device may be relied on, other than what follows from the above.
Results may differ from the reference program's by a relative error of at most 0.00085.
Values sent between devices are 32-bit elements; how exact they have to be, the bound alone decides.
A program may use at most 64 MiB of HBM per device.

```python
import jax
import jax.numpy as jnp
import numpy as np
from jax import lax

EZ = 128
ITERS = 2
NXN = 224
NYN = 56


def draw_forcing(key, part):
    full_shape = (3, NXN, NYN, 7, EZ)
    normal_part = jax.random.truncated_normal(key, -6.0, 6.0, full_shape, jnp.float32)
    position = jnp.arange(NXN, dtype=jnp.float32).reshape(1, NXN, 1, 1, 1) / NXN
    return 10.0 * (1.0 + 2.0 * position) * normal_part


def place_ends(values, stream_key, least, largest):
    dims = values.shape
    place = [jax.random.randint(jax.random.fold_in(stream_key, axis), (), 0, dims[axis]) for axis in range(len(dims))]
    values = values.at[tuple(place)].set(least)
    longest = dims.index(max(dims))
    place[longest] = (place[longest] + 1) % dims[longest]
    return values.at[tuple(place)].set(largest)


def shard_levels(rng, shape, shards, least, top_value):
    def one(dim, shards_of):
        steps = jax.random.uniform(jax.random.fold_in(jax.random.fold_in(rng, 6), dim), (shards_of,), jnp.float32, least / len(shards), top_value / len(shards))
        return jnp.repeat(jnp.exp(steps), shape[dim] // shards_of).reshape((-1,) + (1,) * (len(shape) - dim - 1))

    loudness = one(*shards[0])
    for cut in shards[1:]:
        loudness = loudness * one(*cut)
    return loudness


def centred(rng, shape, scale, bound, pieces=(), held_as=jnp.bfloat16):
    values = jax.random.normal(rng, shape, jnp.float32) * scale
    if len(pieces) > 0:
        values = shard_levels(rng, shape, pieces, -0.22, 0.18) * values
    return jnp.clip(values, min=-bound, max=bound).astype(held_as)


def setup_inputs(seed: int = 0) -> dict:
    streams_of = jax.random.split(jax.random.key(seed), 5)
    forcing = draw_forcing(jax.random.fold_in(streams_of[4], 71), 0)
    initial_guess = centred(streams_of[1], (3, NXN, NYN, 7, EZ), 0.5, 3.0, ((1, 32), (2, 8)), jnp.float32)
    forward_velocity = centred(streams_of[2], (3, NXN, NYN, 7, EZ), 1.0, 4.0, ((1, 32), (2, 8)))
    free_mask = place_ends((jax.random.randint(streams_of[3], (NXN, NYN, 7, EZ), 0, 8) < 7).astype(jnp.int32), jax.random.fold_in(streams_of[3], 1), 0, 1)
    return {"forcing": forcing, "initial_guess": initial_guess, "forward_velocity": forward_velocity, "free_mask": free_mask}


VISC_BASE = 0.5
VISC_GAIN = 0.5
HELMHOLTZ = 20.0


def gll_tables():
    poly_order = 7
    gll_points = np.array([-1.0, -0.8717401485096066153, -0.5917001814331423022, -0.2092992179024788687, 0.2092992179024788687, 0.5917001814331423022, 0.8717401485096066153, 1.0])
    previous = np.ones(8)
    legendre = gll_points.copy()
    for degree in range(1, poly_order):
        following = ((2 * degree + 1) * gll_points * legendre - degree * previous) / (degree + 1)
        previous = legendre
        legendre = following
    quad_weights = 2.0 / (poly_order * (poly_order + 1) * legendre ** 2)
    derivative = np.zeros((8, 8))
    for target in range(8):
        for source in range(8):
            if target != source:
                derivative[target, source] = legendre[target] / legendre[source] / (gll_points[target] - gll_points[source])
    derivative[0, 0] = -poly_order * (poly_order + 1) / 4.0
    derivative[7, 7] = poly_order * (poly_order + 1) / 4.0
    node_weights = quad_weights[:7].copy()
    node_weights[0] = 2.0 * quad_weights[0]
    return quad_weights, derivative, node_weights


def line_weights(length):
    node_weights = gll_tables()[2]
    return jnp.asarray(np.tile(node_weights, length // 7), jnp.float32)


def local_view(values, dimension, elements):
    leading = lax.slice_in_dim(values, 0, 7 * elements, axis=dimension)
    leading = leading.reshape(values.shape[:dimension] + (elements, 7) + values.shape[dimension + 1:])
    closing = lax.slice_in_dim(values, 7, 7 * elements + 1, stride=7, axis=dimension)
    closing = jnp.expand_dims(closing, dimension + 1)
    return jnp.concatenate([leading, closing], axis=dimension + 1)


def fold_view(local_part, dimension, elements):
    leading = lax.slice_in_dim(local_part, 0, 7, axis=dimension + 1)
    out_shape = local_part.shape[:dimension] + (7 * elements,) + local_part.shape[dimension + 2:]
    leading = leading.reshape(out_shape)
    closing = lax.slice_in_dim(local_part, 7, 8, axis=dimension + 1)
    padding = jnp.zeros(closing.shape[:dimension + 1] + (6,) + closing.shape[dimension + 2:], local_part.dtype)
    closing = jnp.concatenate([padding, closing], axis=dimension + 1).reshape(out_shape)
    zero_node = jnp.zeros(out_shape[:dimension] + (1,) + out_shape[dimension + 1:], local_part.dtype)
    return jnp.concatenate([leading, zero_node], axis=dimension) + jnp.concatenate([zero_node, closing], axis=dimension)


def z_view(values):
    first_layer = values[..., 0:1, :]
    return jnp.concatenate([values, jnp.roll(first_layer, -1, axis=-1)], axis=-2)


def z_fold(local_part):
    first_node = local_part[..., 0:1, :] + jnp.roll(local_part[..., 7:8, :], 1, axis=-1)
    return jnp.concatenate([first_node, local_part[..., 1:7, :]], axis=-2)


def kernel(values, coef_part, trailing):
    quad_weights, derivative, node_weights = gll_tables()
    deriv_table = jnp.asarray(derivative, jnp.float32)
    weight_column = jnp.asarray(quad_weights, jnp.float32).reshape((8,) + (1,) * trailing)
    index_tail = "sab"[3 - trailing:]
    gradient = jnp.einsum("mk,...k" + index_tail + "->...m" + index_tail, deriv_table, values, precision=lax.Precision.HIGHEST)
    flux_term = gradient * (weight_column * coef_part)
    return jnp.einsum("mk,...m" + index_tail + "->...k" + index_tail, deriv_table, flux_term, precision=lax.Precision.HIGHEST)


def diag_kernel(coef_part, trailing):
    quad_weights, derivative, node_weights = gll_tables()
    square_table = jnp.asarray(derivative * derivative, jnp.float32)
    weight_column = jnp.asarray(quad_weights, jnp.float32).reshape((8,) + (1,) * trailing)
    index_tail = "sab"[3 - trailing:]
    return jnp.einsum("mk,...m" + index_tail + "->...k" + index_tail, square_table, weight_column * coef_part, precision=lax.Precision.HIGHEST)


def direction_term(values, coef_ext, from_right):
    field_dim = values.ndim - from_right
    coef_dim = coef_ext.ndim - from_right
    elements = (values.shape[field_dim] - 1) // 7
    local_part = kernel(local_view(values, field_dim, elements), local_view(coef_ext, coef_dim, elements), from_right - 1)
    return fold_view(local_part, field_dim, elements)


def diag_term(coef_ext, from_right):
    coef_dim = coef_ext.ndim - from_right
    elements = (coef_ext.shape[coef_dim] - 1) // 7
    return fold_view(diag_kernel(local_view(coef_ext, coef_dim, elements), from_right - 1), coef_dim, elements)


def reference(forcing, initial_guess, forward_velocity, free_mask):
    free_float = free_mask.astype(jnp.float32)
    speed_sq = jnp.sum(jnp.square(forward_velocity.astype(jnp.float32)), axis=0)
    viscosity = VISC_BASE + VISC_GAIN * speed_sq
    weight_x = line_weights(NXN)[:, None, None, None]
    weight_y = line_weights(NYN)[:, None, None]
    weight_z = line_weights(7)[:, None]
    coef_x = viscosity * weight_y * weight_z
    coef_y = viscosity * weight_x * weight_z
    coef_z = viscosity * weight_x * weight_y
    mass_diag = weight_x * weight_y * weight_z * jnp.ones((EZ,), jnp.float32)
    coef_x_ext = jnp.concatenate([coef_x, coef_x[:1]], axis=0)
    coef_y_ext = jnp.concatenate([coef_y, jnp.zeros_like(coef_y[:, :1])], axis=1)
    diag_x = diag_term(coef_x_ext, 4)
    diag_x = jnp.concatenate([diag_x[:1] + diag_x[-1:], diag_x[1:-1]], axis=0)
    diag_y = diag_term(coef_y_ext, 3)[:, :-1]
    diag_z = z_fold(diag_kernel(z_view(coef_z), 1))
    diagonal = diag_x + diag_y + diag_z + HELMHOLTZ * mass_diag

    def operate(values):
        ext_x = jnp.concatenate([values, values[:1]], axis=0)
        term_x = direction_term(ext_x, coef_x_ext, 4)
        term_x = jnp.concatenate([term_x[:1] + term_x[-1:], term_x[1:-1]], axis=0)
        ext_y = jnp.concatenate([values, jnp.zeros_like(values[:, :1])], axis=1)
        term_y = direction_term(ext_y, coef_y_ext, 3)[:, :-1]
        term_z = z_fold(kernel(z_view(values), z_view(coef_z), 1))
        return free_float * (term_x + term_y + term_z + HELMHOLTZ * mass_diag * values)

    def solve_one(component):
        force_part, guess_part = component
        right_side = free_float * mass_diag * force_part
        residual = right_side - operate(guess_part)
        precond = residual / diagonal
        energy_now = jnp.sum(residual * precond)
        direction = precond
        solution = guess_part
        for iteration in range(ITERS):
            applied = operate(direction)
            step_length = energy_now / jnp.sum(direction * applied)
            solution = solution + step_length * direction
            residual = residual - step_length * applied
            precond = residual / diagonal
            energy_next = jnp.sum(residual * precond)
            direction = precond + (energy_next / energy_now) * direction
            energy_now = energy_next
        return solution, direction

    solution, direction = lax.map(solve_one, (forcing, initial_guess))
    return solution, direction
```

```python
import functools

import jax
import jax.numpy as jnp
import numpy as np
from jax import lax
from jax.experimental import pallas as pl
from jax.experimental.pallas import tpu as pltpu
from jax.sharding import PartitionSpec as P

MESH = pl.DeviceIdType.MESH
HELMHOLTZ = 20.0


def gll_tables():
    poly_order = 7
    gll_points = np.array(
        [
            -1.0,
            -0.8717401485096066,
            -0.5917001814331423,
            -0.20929921790247888,
            0.20929921790247888,
            0.5917001814331423,
            0.8717401485096066,
            1.0,
        ]
    )
    previous = np.ones(8)
    legendre = gll_points.copy()
    for degree in range(1, poly_order):
        following = ((2 * degree + 1) * gll_points * legendre - degree * previous) / (degree + 1)
        previous = legendre
        legendre = following
    quad_weights = 2.0 / (poly_order * (poly_order + 1) * legendre**2)
    derivative = np.zeros((8, 8))
    for target in range(8):
        for source in range(8):
            if target != source:
                derivative[target, source] = (
                    legendre[target] / legendre[source] / (gll_points[target] - gll_points[source])
                )
    derivative[0, 0] = -poly_order * (poly_order + 1) / 4.0
    derivative[7, 7] = poly_order * (poly_order + 1) / 4.0
    node_weights = quad_weights[:7].copy()
    node_weights[0] = 2.0 * quad_weights[0]
    return quad_weights, derivative, node_weights


QW, DM, NW = gll_tables()
EVEN = [[float(DM[m, k] + DM[m, 7 - k]) / 2 for k in range(4)] for m in range(4)]
ODD = [[float(DM[m, k] - DM[m, 7 - k]) / 2 for k in range(4)] for m in range(4)]
D77 = float(DM[7, 7])

NZ = 5


def z_constants():
    table = np.zeros((NZ * 8 + 2, 8, 128), np.float32)
    for s in range(NZ):
        for t in range(8):
            for a in range(8):
                m = (a + t) % 8
                table[s * 8 + t, a, :] = DM[m, a] * DM[m, (a + s) % 8]
    for a in range(8):
        table[NZ * 8, a, :] = QW[a]
        table[NZ * 8 + 1, a, :] = NW[a] if a < 7 else 0.0
    return table


def total(terms):
    terms = list(terms)
    while len(terms) > 1:
        terms = [
            terms[i] + terms[i + 1] if i + 1 < len(terms) else terms[i]
            for i in range(0, len(terms), 2)
        ]
    return terms[0]


def by_index(i, table):
    inner = jnp.where((i == 2) | (i == 5), float(table[2]), float(table[3]))
    inner = jnp.where((i == 1) | (i == 6), float(table[1]), inner)
    return jnp.where(i == 0, float(table[0]), inner)


def line_apply(v, kappa):
    p = [v[0]] + [v[j] + v[7 - j] for j in range(1, 4)]
    q = [v[0]] + [v[j] - v[7 - j] for j in range(1, 4)]
    a, b = [], []
    for m in range(4):
        even = total(EVEN[m][k] * p[k] for k in range(4))
        odd = total(ODD[m][k] * q[k] for k in range(4))
        first = kappa[m] * (odd + even)
        last = kappa[7 - m] * (odd - even)
        a.append(first - last)
        b.append(first + last)
    out = [None] * 8
    for k in range(4):
        r = total(EVEN[m][k] * a[m] for m in range(4))
        t = total(ODD[m][k] * b[m] for m in range(4))
        out[k] = r + t
        if k:
            out[7 - k] = r - t
    return out[:7]


def close_rows(tile, last_row):
    moved = pltpu.roll(pltpu.roll(tile, 127, 1), 7, 0)
    return jnp.where(last_row, moved, tile)


def fold_rows(tile, first_row):
    moved = pltpu.roll(pltpu.roll(tile, 1, 1), 1, 0)
    return jnp.where(first_row, tile + moved, tile)


def turned(tile, s):
    return pltpu.roll(tile, 8 - s, 0) if s else tile


def z_apply(closed, diagonals, first_row):
    terms = [diagonals[0] * closed, diagonals[4] * turned(closed, 4)]
    for s in range(1, 4):
        terms.append(diagonals[s] * turned(closed, s))
        terms.append(pltpu.roll(diagonals[s] * closed, s, 0))
    return fold_rows(total(terms), first_row)


def group(px, py, phase):
    x, y, c = px // 8, lax.rem(px // 2, 4), lax.rem(px, 2)
    if phase == 0:
        offsets = [(0, 0, 0, d) for d in (4, 3, 5, 2, 6, 1, 7)]
    else:
        offsets = [
            (dx, dy, dc, 0)
            for dx in (2, 1, 3, 0)
            for dy in (2, 1, 3, 0)
            for dc in (1, 0)
            if dx or dy or dc
        ]
    out = []
    for dx, dy, dc, dz in offsets:
        nx, ny, nc = lax.rem(x + dx, 4), lax.rem(y + dy, 4), lax.rem(c + dc, 2)
        out.append((nx * 8 + ny * 2 + nc, lax.rem(py + dz, 8)))
    return out


GROUPS = (7, 31)


def main_kernel(
    f_hbm, x_hbm, fv_hbm, m_hbm, z_hbm,
    v1, v2, v3, coef,
    f7, x7, fv7, m7, zc, v0, fm, cv, acc, kx, ky, bx, by, zd, mdi, dg,
    s_out, rv, rs, rb, row_out, rows_in,
    load_sem, send_sem, recv_sem, set_send, set_recv, row_send, row_recv,
):
    px = lax.axis_index("px")
    py = lax.axis_index("py")
    not_first = py > 0
    not_last = py < 7
    prev_x, next_x = (lax.rem(px + 31, 32), py), (lax.rem(px + 1, 32), py)
    prev_y, next_y = (px, lax.rem(py + 7, 8)), (px, lax.rem(py + 1, 8))

    loads = [
        pltpu.make_async_copy(src, dst, load_sem.at[i])
        for i, (src, dst) in enumerate(
            ((fv_hbm, fv7), (x_hbm, x7), (f_hbm, f7), (z_hbm, zc), (m_hbm, m7))
        )
    ]
    for load in loads:
        load.start()

    partners = [group(px, py, phase) for phase in (0, 1)]
    barrier = pltpu.get_barrier_semaphore()
    for device in partners[1] + partners[0]:
        pl.semaphore_signal(barrier, inc=1, device_id=device, device_id_type=MESH)

    zero_row = jnp.zeros((1, 128), jnp.float32)
    zero_face = jnp.zeros((7, 8, 128), jnp.float32)

    @pl.when(py == 0)
    def _():
        rb[1] = zero_face
        for r in range(3):
            for c in range(3):
                rs[r, c, 1, 0] = zero_face
                rs[r, c, 1, 1] = zero_face

    @pl.when(py == 7)
    def _():
        ky[:, 7] = zero_face
        for r in range(3):
            for c in range(3):
                rv[r, c, 1] = zero_face

    rows = lax.broadcasted_iota(jnp.int32, (8, 128), 0)
    lanes = lax.broadcasted_iota(jnp.int32, (8, 128), 1)
    first_row, last_row = rows == 0, rows == 7
    each = functools.partial(lax.fori_loop, 0, 7)

    loads[0].wait()

    def viscosity(x, carry):
        for y in range(7):
            speed = [fv7[i, x, y].astype(jnp.float32) for i in range(3)]
            cv[x, y, 0:7, :] = 0.5 + 0.5 * (
                speed[0] * speed[0] + speed[1] * speed[1] + speed[2] * speed[2]
            )
            cv[x, y, 7:8, :] = zero_row
        return carry

    each(viscosity, 0)
    loads[3].wait()
    nwa = zc[NZ * 8 + 1]

    def coefficients(x, carry):
        wx, nwx = by_index(x, QW), by_index(x, NW)
        for y in range(7):
            base = cv[x, y] * nwa
            kx[x, y] = base * (wx * float(NW[y]))
            ky[x, y] = base * (nwx * float(QW[y]))
        return carry

    each(coefficients, 0)

    def remote(src, dst, send, recv, device):
        return pltpu.make_async_remote_copy(
            src_ref=src,
            dst_ref=dst,
            send_sem=send,
            recv_sem=recv,
            device_id=device,
            device_id_type=MESH,
        )

    setup_copies = [
        remote(kx.at[0], kx.at[7], set_send.at[0], set_recv.at[0], prev_x),
        remote(ky.at[:, 0], ky.at[:, 7], set_send.at[1], set_recv.at[1], prev_y),
        remote(bx.at[7], rb.at[0], set_send.at[2], set_recv.at[2], next_x),
        remote(by.at[:, 7], rb.at[1], set_send.at[3], set_recv.at[3], next_y),
    ]
    vecs = (v0, v1, v2, v3)

    def face_copies(r, c):
        extra = 2 if r == 0 else 1
        v = vecs[r]
        ends = (
            (v.at[c, 0], rv.at[r, c, 0], prev_x),
            (v.at[c, :, 0], rv.at[r, c, 1], prev_y),
            (s_out.at[r, c, 0, 0:extra], rs.at[r, c, 0, 0:extra], next_x),
            (s_out.at[r, c, 1, 0:extra], rs.at[r, c, 1, 0:extra], next_y),
        )
        return [
            remote(src, dst, send_sem.at[r, c, i], recv_sem.at[r, c, i], device)
            for i, (src, dst, device) in enumerate(ends)
        ]

    def start(copies):
        copies[0].start()
        pl.when(not_first)(copies[1].start)
        copies[2].start()
        pl.when(not_last)(copies[3].start)

    def wait_recv(copies):
        copies[0].wait_recv()
        pl.when(not_last)(copies[1].wait_recv)
        copies[2].wait_recv()
        pl.when(not_first)(copies[3].wait_recv)

    def wait_send(copies):
        copies[0].wait_send()
        pl.when(not_first)(copies[1].wait_send)
        copies[2].wait_send()
        pl.when(not_last)(copies[3].wait_send)

    pl.semaphore_wait(barrier, sum(GROUPS))
    setup_copies[0].start()
    pl.when(not_first)(setup_copies[1].start)

    def last_rows(i, carry):
        along_x = [kx[m, i] for m in range(7)]
        for k in range(8):
            bx[k, i] = total(float(DM[m, k] * DM[m, 7]) * along_x[m] for m in range(7))
        along_y = [ky[i, m] for m in range(7)]
        for k in range(8):
            by[i, k] = total(float(DM[m, k] * DM[m, 7]) * along_y[m] for m in range(7))
        return carry

    each(last_rows, 0)
    setup_copies[2].start()
    pl.when(not_last)(setup_copies[3].start)

    loads[1].wait()
    loads[2].wait()

    def spread_inputs(x, carry):
        nwx = by_index(x, NW)
        for c in range(3):
            for y in range(7):
                v0[c, x, y, 0:7, :] = x7[c, x, y]
                v0[c, x, y, 7:8, :] = zero_row
                fm[c, x, y, 0:7, :] = f7[c, x, y] * (nwa[0:7] * (nwx * float(NW[y])))
                fm[c, x, y, 7:8, :] = zero_row
        return carry

    each(spread_inputs, 0)

    for c in range(3):

        def first_sums(i, carry, c=c):
            v = [v0[c, k, i] for k in range(7)]
            s_out[0, c, 0, 0, i] = total(bx[k, i] * v[k] for k in range(7))
            s_out[0, c, 0, 1, i] = total(float(DM[7, k]) * v[k] for k in range(7))
            v = [v0[c, i, k] for k in range(7)]
            s_out[0, c, 1, 0, i] = total(by[i, k] * v[k] for k in range(7))
            s_out[0, c, 1, 1, i] = total(float(DM[7, k]) * v[k] for k in range(7))
            return carry

        each(first_sums, 0)
        start(face_copies(0, c))

    wz = zc[NZ * 8]

    def z_setup(x, carry):
        nwx = by_index(x, NW)
        for y in range(7):
            kz = close_rows(cv[x, y], last_row) * (wz * (nwx * float(NW[y])))
            turns = [turned(kz, t) for t in range(8)]
            for s in range(NZ):
                value = total(zc[s * 8 + t] * turns[t] for t in range(8))
                if s == 0:
                    value = value + nwa * (nwx * float(HELMHOLTZ * NW[y]))
                zd[x, y, s] = value
        return carry

    each(z_setup, 0)

    loads[4].wait()
    setup_copies[0].wait_recv()
    pl.when(not_last)(setup_copies[1].wait_recv)
    setup_copies[2].wait_recv()
    pl.when(not_first)(setup_copies[3].wait_recv)
    setup_copies[2].wait_send()
    pl.when(not_last)(setup_copies[3].wait_send)
    inner_y = jnp.where(not_first, D77 * D77, 0.0)

    def first_layers(i, carry):
        zd[0, i, 0] = zd[0, i, 0] + (rb[0, i] + (D77 * D77) * kx[0, i])
        zd[i, 0, 0] = zd[i, 0, 0] + (rb[1, i] + inner_y * ky[i, 0])
        return carry

    each(first_layers, 0)

    def x_diagonal(y, carry):
        kappa = [kx[m, y] for m in range(8)]
        for k in range(7):
            dg[k, y] = total(float(DM[m, k] ** 2) * kappa[m] for m in range(8))
            bx[k, y] = bx[k, y] + float(DM[7, k] * D77) * kappa[7]
        return carry

    each(x_diagonal, 0)

    def y_diagonal(x, carry):
        kappa = [ky[x, m] for m in range(8)]
        for k in range(7):
            value = total(float(DM[m, k] ** 2) * kappa[m] for m in range(8))
            by[x, k] = by[x, k] + float(DM[7, k] * D77) * kappa[7]
            value = value + dg[x, k] + fold_rows(zd[x, k, 0], first_row)
            value = jnp.where(last_row, 1.0, value)
            dg[x, k] = value
            mdi[x, k, 0:7, :] = m7[x, k].astype(jnp.float32) / value[0:7]
            mdi[x, k, 7:8, :] = zero_row
        return carry

    each(y_diagonal, 0)

    def local_apply(r):
        v_ref = vecs[r]
        for c in range(3):

            def x_lines(y, carry, c=c):
                out = line_apply([v_ref[c, k, y] for k in range(7)], [kx[m, y] for m in range(8)])
                for k in range(7):
                    acc[c, k, y] = out[k]
                return carry

            each(x_lines, 0)

            def yz_lines(x, carry, c=c):
                v = [v_ref[c, x, k] for k in range(7)]
                out = line_apply(v, [ky[x, m] for m in range(8)])
                for k in range(7):
                    z_part = z_apply(
                        close_rows(v[k], last_row), [zd[x, k, s] for s in range(NZ)], first_row
                    )
                    acc[c, x, k] = acc[c, x, k] + out[k] + z_part
                return carry

            each(yz_lines, 0)

    zero_tile = jnp.zeros((8, 128), jnp.float32)
    moments = {}

    def finish(r, c):
        v_ref, u_ref = vecs[r], vecs[r + 1]
        for i in range(7):
            sum_x, sum_y = rs[r, c, 0, 0, i], rs[r, c, 1, 0, i]
            if r == 0:
                sum_x = sum_x + D77 * kx[0, i] * rs[r, c, 0, 1, i]
                sum_y = sum_y + D77 * ky[i, 0] * rs[r, c, 1, 1, i]
            acc[c, 0, i] = acc[c, 0, i] + sum_x
            acc[c, i, 0] = acc[c, i, 0] + sum_y

        def row(x, carry):
            sums, tally = carry
            sums, tally = list(sums), list(tally)
            end_y = rv[r, c, 1, x]
            sum_y = []
            for y in range(7):
                b_x, b_y = bx[x, y], by[x, y]
                t = acc[c, x, y] + b_x * rv[r, c, 0, y] + b_y * end_y
                if r == 0:
                    u = mdi[x, y] * (fm[c, x, y] - t)
                else:
                    v = v_ref[c, x, y]
                    u = v - mdi[x, y] * t
                u_ref[c, x, y] = u
                if r < 2:
                    sums[y] = sums[y] + b_x * u
                    sum_y.append(b_y * u)
                weighted = dg[x, y] * u
                if r:
                    tally[0] = tally[0] + v * weighted
                tally[1] = tally[1] + u * weighted
            if r < 2:
                s_out[r + 1, c, 1, 0, x] = total(sum_y)
            return tuple(sums), tuple(tally)

        sums, tally = each(row, ((zero_tile,) * (7 if r < 2 else 0), (zero_tile,) * 2))
        if r < 2:
            for y in range(7):
                s_out[r + 1, c, 0, 0, y] = sums[y]
        if r:
            moments[2 * r - 1, c] = tally[0]
        moments[2 * r, c] = tally[1]

    for r in range(3):
        local_apply(r)
        for c in range(3):
            wait_recv(face_copies(r, c))
            finish(r, c)
            if r < 2:
                start(face_copies(r + 1, c))

    halves = []
    for half in range(2):
        stack = zero_tile
        for j in range(8):
            index = half * 8 + j
            if index < 15:
                value = jnp.sum(moments[index // 3, index % 3], axis=0, keepdims=True)
                stack = jnp.where(rows == j, value, stack)
        value = jnp.sum(stack, axis=1, keepdims=True)
        halves.append(jnp.where(lanes == rows + 8 * half, value, 0.0))
    row_total = jnp.sum(halves[0] + halves[1], axis=0, keepdims=True)

    for phase in range(2):
        count = GROUPS[phase]
        row_out[phase] = row_total
        for slot, device in enumerate(partners[phase]):
            remote(
                row_out.at[phase],
                rows_in.at[phase, slot],
                row_send.at[phase],
                row_recv.at[phase],
                device,
            ).start()
        everything = rows_in.at[phase, pl.ds(0, count)]
        pltpu.make_async_copy(everything, everything, row_recv.at[phase]).wait()
        row_total = total([row_total] + [rows_in[phase, slot] for slot in range(count)])

    n = []
    for k in range(5):
        picked = jnp.where(lanes == rows + 3 * k, jnp.broadcast_to(row_total, (8, 128)), 0.0)
        n.append(jnp.broadcast_to(jnp.sum(picked, axis=1, keepdims=True), (8, 128)))
    alpha0 = n[0] / (n[0] - n[1])
    a = -n[1] / (n[0] - n[1])
    e1 = a * a * n[0] + 2.0 * a * alpha0 * n[1] + alpha0 * alpha0 * n[2]
    b = a + e1 / n[0]
    curvature = (
        b * b * (n[0] - n[1]) + 2.0 * b * alpha0 * (n[1] - n[2]) + alpha0 * alpha0 * (n[2] - n[3])
    )
    alpha1 = e1 / curvature
    a0 = a - alpha1 * b
    a1 = alpha0 - alpha1 * (alpha0 - b)
    a2 = alpha1 * alpha0
    e2 = (
        a0 * a0 * n[0]
        + 2.0 * a0 * a1 * n[1]
        + (a1 * a1 + 2.0 * a0 * a2) * n[2]
        + 2.0 * a1 * a2 * n[3]
        + a2 * a2 * n[4]
    )
    beta1 = e2 / e1
    coef[0] = alpha0 + alpha1 * b
    coef[1] = a2
    coef[2] = a0 + beta1 * b
    coef[3] = a1 + beta1 * alpha0
    coef[4] = a2

    setup_copies[0].wait_send()
    pl.when(not_first)(setup_copies[1].wait_send)
    for r in range(3):
        for c in range(3):
            wait_send(face_copies(r, c))
    for phase in range(2):
        everything = rows_in.at[phase, pl.ds(0, GROUPS[phase])]
        pltpu.make_async_copy(everything, everything, row_send.at[phase]).wait()


def body(forcing, initial_guess, forward_velocity, free_mask):
    field = (3, 7, 7, 8, 128)
    plane = (7, 7, 8, 128)
    f32 = jnp.float32
    hbm = pl.BlockSpec(memory_space=pl.ANY)
    vmem = pl.BlockSpec(memory_space=pltpu.VMEM)
    v1, v2, v3, coef = pl.pallas_call(
        main_kernel,
        out_shape=[jax.ShapeDtypeStruct(field, f32)] * 3
        + [jax.ShapeDtypeStruct((5, 8, 128), f32)],
        in_specs=[hbm] * 5,
        out_specs=[vmem] * 4,
        scratch_shapes=[
            pltpu.VMEM((3, 7, 7, 7, 128), f32),
            pltpu.VMEM((3, 7, 7, 7, 128), f32),
            pltpu.VMEM((3, 7, 7, 7, 128), jnp.bfloat16),
            pltpu.VMEM((7, 7, 7, 128), jnp.int32),
            pltpu.VMEM((NZ * 8 + 2, 8, 128), f32),
            pltpu.VMEM(field, f32),
            pltpu.VMEM(field, f32),
            pltpu.VMEM(plane, f32),
            pltpu.VMEM(field, f32),
            pltpu.VMEM((8, 7, 8, 128), f32),
            pltpu.VMEM((7, 8, 8, 128), f32),
            pltpu.VMEM((8, 7, 8, 128), f32),
            pltpu.VMEM((7, 8, 8, 128), f32),
            pltpu.VMEM((7, 7, NZ, 8, 128), f32),
            pltpu.VMEM(plane, f32),
            pltpu.VMEM(plane, f32),
            pltpu.VMEM((3, 3, 2, 2, 7, 8, 128), f32),
            pltpu.VMEM((3, 3, 2, 7, 8, 128), f32),
            pltpu.VMEM((3, 3, 2, 2, 7, 8, 128), f32),
            pltpu.VMEM((2, 7, 8, 128), f32),
            pltpu.VMEM((2, 1, 128), f32),
            pltpu.VMEM((2, 31, 1, 128), f32),
            pltpu.SemaphoreType.DMA((5,)),
            pltpu.SemaphoreType.DMA((3, 3, 4)),
            pltpu.SemaphoreType.DMA((3, 3, 4)),
            pltpu.SemaphoreType.DMA((4,)),
            pltpu.SemaphoreType.DMA((4,)),
            pltpu.SemaphoreType.DMA((2,)),
            pltpu.SemaphoreType.DMA((2,)),
        ],
        compiler_params=pltpu.CompilerParams(
            collective_id=0, has_side_effects=True, vmem_limit_bytes=32 << 20
        ),
    )(forcing, initial_guess, forward_velocity, free_mask, jnp.asarray(z_constants()))
    v1, v2, v3 = (v[..., :7, :] for v in (v1, v2, v3))
    coef = coef[:, :3, None, None, None, :]
    guess = initial_guess + coef[0] * v1 + coef[1] * v2
    direction = coef[2] * v1 + coef[3] * v2 + coef[4] * v3
    return guess, direction


def solution(mesh):
    placed = (
        P(None, "px", "py", None, None),
        P(None, "px", "py", None, None),
        P(None, "px", "py", None, None),
        P("px", "py", None, None),
    )
    return jax.shard_map(
        body,
        mesh=mesh,
        in_specs=placed,
        out_specs=(P(None, "px", "py", None, None), P(None, "px", "py", None, None)),
        check_vma=False,
    )
```

```python
import functools

import jax
import jax.numpy as jnp
import numpy as np
from jax import lax
from jax.experimental import pallas as pl
from jax.experimental.pallas import tpu as pltpu
from jax.sharding import PartitionSpec as P

MESH = pl.DeviceIdType.MESH
HELMHOLTZ = 20.0


def gll_tables():
    poly_order = 7
    gll_points = np.array(
        [
            -1.0,
            -0.8717401485096066,
            -0.5917001814331423,
            -0.20929921790247888,
            0.20929921790247888,
            0.5917001814331423,
            0.8717401485096066,
            1.0,
        ]
    )
    previous = np.ones(8)
    legendre = gll_points.copy()
    for degree in range(1, poly_order):
        following = ((2 * degree + 1) * gll_points * legendre - degree * previous) / (degree + 1)
        previous = legendre
        legendre = following
    quad_weights = 2.0 / (poly_order * (poly_order + 1) * legendre**2)
    derivative = np.zeros((8, 8))
    for target in range(8):
        for source in range(8):
            if target != source:
                derivative[target, source] = (
                    legendre[target] / legendre[source] / (gll_points[target] - gll_points[source])
                )
    derivative[0, 0] = -poly_order * (poly_order + 1) / 4.0
    derivative[7, 7] = poly_order * (poly_order + 1) / 4.0
    node_weights = quad_weights[:7].copy()
    node_weights[0] = 2.0 * quad_weights[0]
    return quad_weights, derivative, node_weights


QW, DM, NW = gll_tables()
EVEN = [[float(DM[m, k] + DM[m, 7 - k]) / 2 for k in range(4)] for m in range(4)]
ODD = [[float(DM[m, k] - DM[m, 7 - k]) / 2 for k in range(4)] for m in range(4)]
D77 = float(DM[7, 7])

NZ = 5


def z_constants():
    table = np.zeros((NZ * 8 + 2, 8, 128), np.float32)
    for s in range(NZ):
        for t in range(8):
            for a in range(8):
                m = (a + t) % 8
                table[s * 8 + t, a, :] = DM[m, a] * DM[m, (a + s) % 8]
    for a in range(8):
        table[NZ * 8, a, :] = QW[a]
        table[NZ * 8 + 1, a, :] = NW[a] if a < 7 else 0.0
    return table


def total(terms):
    terms = list(terms)
    while len(terms) > 1:
        terms = [
            terms[i] + terms[i + 1] if i + 1 < len(terms) else terms[i]
            for i in range(0, len(terms), 2)
        ]
    return terms[0]


def by_index(i, table):
    inner = jnp.where((i == 2) | (i == 5), float(table[2]), float(table[3]))
    inner = jnp.where((i == 1) | (i == 6), float(table[1]), inner)
    return jnp.where(i == 0, float(table[0]), inner)


def line_apply(v, kappa):
    p = [v[0]] + [v[j] + v[7 - j] for j in range(1, 4)]
    q = [v[0]] + [v[j] - v[7 - j] for j in range(1, 4)]
    a, b = [], []
    for m in range(4):
        even = total(EVEN[m][k] * p[k] for k in range(4))
        odd = total(ODD[m][k] * q[k] for k in range(4))
        first = kappa[m] * (odd + even)
        last = kappa[7 - m] * (odd - even)
        a.append(first - last)
        b.append(first + last)
    out = [None] * 8
    for k in range(4):
        r = total(EVEN[m][k] * a[m] for m in range(4))
        t = total(ODD[m][k] * b[m] for m in range(4))
        out[k] = r + t
        if k:
            out[7 - k] = r - t
    return out[:7]


def close_rows(tile, last_row):
    moved = pltpu.roll(pltpu.roll(tile, 127, 1), 7, 0)
    return jnp.where(last_row, moved, tile)


def fold_rows(tile, first_row):
    moved = pltpu.roll(pltpu.roll(tile, 1, 1), 1, 0)
    return jnp.where(first_row, tile + moved, tile)


def turned(tile, s):
    return pltpu.roll(tile, 8 - s, 0) if s else tile


def z_apply(closed, diagonals, first_row):
    terms = [diagonals[0] * closed, diagonals[4] * turned(closed, 4)]
    for s in range(1, 4):
        terms.append(diagonals[s] * turned(closed, s))
        terms.append(pltpu.roll(diagonals[s] * closed, s, 0))
    return fold_rows(total(terms), first_row)


def group(px, py, phase):
    x, y, c = px // 8, lax.rem(px // 2, 4), lax.rem(px, 2)
    if phase == 0:
        offsets = [(0, 0, 0, d) for d in (4, 3, 5, 2, 6, 1, 7)]
    else:
        offsets = [
            (dx, dy, dc, 0)
            for dx in (2, 1, 3, 0)
            for dy in (2, 1, 3, 0)
            for dc in (1, 0)
            if dx or dy or dc
        ]
    out = []
    for dx, dy, dc, dz in offsets:
        nx, ny, nc = lax.rem(x + dx, 4), lax.rem(y + dy, 4), lax.rem(c + dc, 2)
        out.append((nx * 8 + ny * 2 + nc, lax.rem(py + dz, 8)))
    return out


GROUPS = (7, 31)


def main_kernel(
    f_hbm, x_hbm, fv_hbm, m_hbm, z_hbm,
    v1, v2, v3, coef,
    f7, x7, fv7, m7, zc, v0, fm, cv, acc, kx, ky, bx, by, zd, mdi, dg,
    s_out, rv, rs, rb, row_out, rows_in,
    load_sem, send_sem, recv_sem, set_send, set_recv, row_send, row_recv,
):
    px = lax.axis_index("px")
    py = lax.axis_index("py")
    not_first = py > 0
    not_last = py < 7
    prev_x, next_x = (lax.rem(px + 31, 32), py), (lax.rem(px + 1, 32), py)
    prev_y, next_y = (px, lax.rem(py + 7, 8)), (px, lax.rem(py + 1, 8))

    loads = [
        pltpu.make_async_copy(src, dst, load_sem.at[i])
        for i, (src, dst) in enumerate(
            ((fv_hbm, fv7), (x_hbm, x7), (f_hbm, f7), (z_hbm, zc), (m_hbm, m7))
        )
    ]
    for load in loads:
        load.start()

    partners = [group(px, py, phase) for phase in (0, 1)]
    barrier = pltpu.get_barrier_semaphore()
    for device in partners[1] + partners[0]:
        pl.semaphore_signal(barrier, inc=1, device_id=device, device_id_type=MESH)

    zero_row = jnp.zeros((1, 128), jnp.float32)
    zero_face = jnp.zeros((7, 8, 128), jnp.float32)

    @pl.when(py == 0)
    def _():
        rb[1] = zero_face
        for r in range(3):
            for c in range(3):
                rs[r, c, 1, 0] = zero_face
                rs[r, c, 1, 1] = zero_face

    @pl.when(py == 7)
    def _():
        ky[:, 7] = zero_face
        for r in range(3):
            for c in range(3):
                rv[r, c, 1] = zero_face

    rows = lax.broadcasted_iota(jnp.int32, (8, 128), 0)
    lanes = lax.broadcasted_iota(jnp.int32, (8, 128), 1)
    first_row, last_row = rows == 0, rows == 7
    each = functools.partial(lax.fori_loop, 0, 7)

    loads[0].wait()

    def viscosity(x, carry):
        for y in range(7):
            speed = [fv7[i, x, y].astype(jnp.float32) for i in range(3)]
            cv[x, y, 0:7, :] = 0.5 + 0.5 * (
                speed[0] * speed[0] + speed[1] * speed[1] + speed[2] * speed[2]
            )
            cv[x, y, 7:8, :] = zero_row
        return carry

    each(viscosity, 0)
    loads[3].wait()
    nwa = zc[NZ * 8 + 1]

    def coefficients(x, carry):
        wx, nwx = by_index(x, QW), by_index(x, NW)
        for y in range(7):
            base = cv[x, y] * nwa
            kx[x, y] = base * (wx * float(NW[y]))
            ky[x, y] = base * (nwx * float(QW[y]))
        return carry

    each(coefficients, 0)

    def remote(src, dst, send, recv, device):
        return pltpu.make_async_remote_copy(
            src_ref=src,
            dst_ref=dst,
            send_sem=send,
            recv_sem=recv,
            device_id=device,
            device_id_type=MESH,
        )

    setup_copies = [
        remote(kx.at[0], kx.at[7], set_send.at[0], set_recv.at[0], prev_x),
        remote(ky.at[:, 0], ky.at[:, 7], set_send.at[1], set_recv.at[1], prev_y),
        remote(bx.at[7], rb.at[0], set_send.at[2], set_recv.at[2], next_x),
        remote(by.at[:, 7], rb.at[1], set_send.at[3], set_recv.at[3], next_y),
    ]
    vecs = (v0, v1, v2, v3)

    def face_copies(r, c):
        extra = 2 if r == 0 else 1
        v = vecs[r]
        ends = (
            (v.at[c, 0], rv.at[r, c, 0], prev_x),
            (v.at[c, :, 0], rv.at[r, c, 1], prev_y),
            (s_out.at[r, c, 0, 0:extra], rs.at[r, c, 0, 0:extra], next_x),
            (s_out.at[r, c, 1, 0:extra], rs.at[r, c, 1, 0:extra], next_y),
        )
        return [
            remote(src, dst, send_sem.at[r, c, i], recv_sem.at[r, c, i], device)
            for i, (src, dst, device) in enumerate(ends)
        ]

    def start(copies):
        copies[0].start()
        pl.when(not_first)(copies[1].start)
        copies[2].start()
        pl.when(not_last)(copies[3].start)

    def wait_recv(copies):
        copies[0].wait_recv()
        pl.when(not_last)(copies[1].wait_recv)
        copies[2].wait_recv()
        pl.when(not_first)(copies[3].wait_recv)

    def wait_send(copies):
        copies[0].wait_send()
        pl.when(not_first)(copies[1].wait_send)
        copies[2].wait_send()
        pl.when(not_last)(copies[3].wait_send)

    pl.semaphore_wait(barrier, sum(GROUPS))
    setup_copies[0].start()
    pl.when(not_first)(setup_copies[1].start)

    def last_rows(i, carry):
        along_x = [kx[m, i] for m in range(7)]
        for k in range(8):
            bx[k, i] = total(float(DM[m, k] * DM[m, 7]) * along_x[m] for m in range(7))
        along_y = [ky[i, m] for m in range(7)]
        for k in range(8):
            by[i, k] = total(float(DM[m, k] * DM[m, 7]) * along_y[m] for m in range(7))
        return carry

    each(last_rows, 0)
    setup_copies[2].start()
    pl.when(not_last)(setup_copies[3].start)

    loads[1].wait()
    loads[2].wait()

    def spread_inputs(x, carry):
        nwx = by_index(x, NW)
        for c in range(3):
            for y in range(7):
                v0[c, x, y, 0:7, :] = x7[c, x, y]
                v0[c, x, y, 7:8, :] = zero_row
                fm[c, x, y, 0:7, :] = f7[c, x, y] * (nwa[0:7] * (nwx * float(NW[y])))
                fm[c, x, y, 7:8, :] = zero_row
        return carry

    each(spread_inputs, 0)

    for c in range(3):

        def first_sums(i, carry, c=c):
            v = [v0[c, k, i] for k in range(7)]
            s_out[0, c, 0, 0, i] = total(bx[k, i] * v[k] for k in range(7))
            s_out[0, c, 0, 1, i] = total(float(DM[7, k]) * v[k] for k in range(7))
            v = [v0[c, i, k] for k in range(7)]
            s_out[0, c, 1, 0, i] = total(by[i, k] * v[k] for k in range(7))
            s_out[0, c, 1, 1, i] = total(float(DM[7, k]) * v[k] for k in range(7))
            return carry

        each(first_sums, 0)
        start(face_copies(0, c))

    wz = zc[NZ * 8]

    def z_setup(x, carry):
        nwx = by_index(x, NW)
        for y in range(7):
            kz = close_rows(cv[x, y], last_row) * (wz * (nwx * float(NW[y])))
            turns = [turned(kz, t) for t in range(8)]
            for s in range(NZ):
                value = total(zc[s * 8 + t] * turns[t] for t in range(8))
                if s == 0:
                    value = value + nwa * (nwx * float(HELMHOLTZ * NW[y]))
                zd[x, y, s] = value
        return carry

    each(z_setup, 0)

    loads[4].wait()
    setup_copies[0].wait_recv()
    pl.when(not_last)(setup_copies[1].wait_recv)
    setup_copies[2].wait_recv()
    pl.when(not_first)(setup_copies[3].wait_recv)
    setup_copies[2].wait_send()
    pl.when(not_last)(setup_copies[3].wait_send)
    inner_y = jnp.where(not_first, D77 * D77, 0.0)

    def first_layers(i, carry):
        zd[0, i, 0] = zd[0, i, 0] + (rb[0, i] + (D77 * D77) * kx[0, i])
        zd[i, 0, 0] = zd[i, 0, 0] + (rb[1, i] + inner_y * ky[i, 0])
        return carry

    each(first_layers, 0)

    def x_diagonal(y, carry):
        kappa = [kx[m, y] for m in range(8)]
        for k in range(7):
            dg[k, y] = total(float(DM[m, k] ** 2) * kappa[m] for m in range(8))
            bx[k, y] = bx[k, y] + float(DM[7, k] * D77) * kappa[7]
        return carry

    each(x_diagonal, 0)

    def y_diagonal(x, carry):
        kappa = [ky[x, m] for m in range(8)]
        for k in range(7):
            value = total(float(DM[m, k] ** 2) * kappa[m] for m in range(8))
            by[x, k] = by[x, k] + float(DM[7, k] * D77) * kappa[7]
            value = value + dg[x, k] + fold_rows(zd[x, k, 0], first_row)
            value = jnp.where(last_row, 1.0, value)
            dg[x, k] = value
            mdi[x, k, 0:7, :] = m7[x, k].astype(jnp.float32) / value[0:7]
            mdi[x, k, 7:8, :] = zero_row
        return carry

    each(y_diagonal, 0)

    def local_apply(r):
        v_ref = vecs[r]
        for c in range(3):

            def x_lines(y, carry, c=c):
                out = line_apply([v_ref[c, k, y] for k in range(7)], [kx[m, y] for m in range(8)])
                for k in range(7):
                    acc[c, k, y] = out[k]
                return carry

            each(x_lines, 0)

            def yz_lines(x, carry, c=c):
                v = [v_ref[c, x, k] for k in range(7)]
                out = line_apply(v, [ky[x, m] for m in range(8)])
                for k in range(7):
                    z_part = z_apply(
                        close_rows(v[k], last_row), [zd[x, k, s] for s in range(NZ)], first_row
                    )
                    acc[c, x, k] = acc[c, x, k] + out[k] + z_part
                return carry

            each(yz_lines, 0)

    zero_tile = jnp.zeros((8, 128), jnp.float32)
    moments = {}

    def finish(r, c):
        v_ref, u_ref = vecs[r], vecs[r + 1]
        for i in range(7):
            sum_x, sum_y = rs[r, c, 0, 0, i], rs[r, c, 1, 0, i]
            if r == 0:
                sum_x = sum_x + D77 * kx[0, i] * rs[r, c, 0, 1, i]
                sum_y = sum_y + D77 * ky[i, 0] * rs[r, c, 1, 1, i]
            acc[c, 0, i] = acc[c, 0, i] + sum_x
            acc[c, i, 0] = acc[c, i, 0] + sum_y

        def row(x, carry):
            sums, tally = carry
            sums, tally = list(sums), list(tally)
            end_y = rv[r, c, 1, x]
            sum_y = []
            for y in range(7):
                b_x, b_y = bx[x, y], by[x, y]
                t = acc[c, x, y] + b_x * rv[r, c, 0, y] + b_y * end_y
                if r == 0:
                    u = mdi[x, y] * (fm[c, x, y] - t)
                else:
                    v = v_ref[c, x, y]
                    u = v - mdi[x, y] * t
                u_ref[c, x, y] = u
                if r < 2:
                    sums[y] = sums[y] + b_x * u
                    sum_y.append(b_y * u)
                weighted = dg[x, y] * u
                if r:
                    tally[0] = tally[0] + v * weighted
                tally[1] = tally[1] + u * weighted
            if r < 2:
                s_out[r + 1, c, 1, 0, x] = total(sum_y)
            return tuple(sums), tuple(tally)

        sums, tally = each(row, ((zero_tile,) * (7 if r < 2 else 0), (zero_tile,) * 2))
        if r < 2:
            for y in range(7):
                s_out[r + 1, c, 0, 0, y] = sums[y]
        if r:
            moments[2 * r - 1, c] = tally[0]
        moments[2 * r, c] = tally[1]

    for r in range(3):
        local_apply(r)
        for c in range(3):
            wait_recv(face_copies(r, c))
            finish(r, c)
            if r < 2:
                start(face_copies(r + 1, c))

    halves = []
    for half in range(2):
        stack = zero_tile
        for j in range(8):
            index = half * 8 + j
            if index < 15:
                value = jnp.sum(moments[index // 3, index % 3], axis=0, keepdims=True)
                stack = jnp.where(rows == j, value, stack)
        value = jnp.sum(stack, axis=1, keepdims=True)
        halves.append(jnp.where(lanes == rows + 8 * half, value, 0.0))
    row_total = jnp.sum(halves[0] + halves[1], axis=0, keepdims=True)

    for phase in range(2):
        count = GROUPS[phase]
        row_out[phase] = row_total
        for slot, device in enumerate(partners[phase]):
            remote(
                row_out.at[phase],
                rows_in.at[phase, slot],
                row_send.at[phase],
                row_recv.at[phase],
                device,
            ).start()
        everything = rows_in.at[phase, pl.ds(0, count)]
        pltpu.make_async_copy(everything, everything, row_recv.at[phase]).wait()
        row_total = total([row_total] + [rows_in[phase, slot] for slot in range(count)])

    n = []
    for k in range(5):
        picked = jnp.where(lanes == rows + 3 * k, jnp.broadcast_to(row_total, (8, 128)), 0.0)
        n.append(jnp.broadcast_to(jnp.sum(picked, axis=1, keepdims=True), (8, 128)))
    alpha0 = n[0] / (n[0] - n[1])
    a = -n[1] / (n[0] - n[1])
    e1 = a * a * n[0] + 2.0 * a * alpha0 * n[1] + alpha0 * alpha0 * n[2]
    b = a + e1 / n[0]
    curvature = (
        b * b * (n[0] - n[1]) + 2.0 * b * alpha0 * (n[1] - n[2]) + alpha0 * alpha0 * (n[2] - n[3])
    )
    alpha1 = e1 / curvature
    a0 = a - alpha1 * b
    a1 = alpha0 - alpha1 * (alpha0 - b)
    a2 = alpha1 * alpha0
    e2 = (
        a0 * a0 * n[0]
        + 2.0 * a0 * a1 * n[1]
        + (a1 * a1 + 2.0 * a0 * a2) * n[2]
        + 2.0 * a1 * a2 * n[3]
        + a2 * a2 * n[4]
    )
    beta1 = e2 / e1
    coef[0] = alpha0 + alpha1 * b
    coef[1] = a2
    coef[2] = a0 + beta1 * b
    coef[3] = a1 + beta1 * alpha0
    coef[4] = a2

    setup_copies[0].wait_send()
    pl.when(not_first)(setup_copies[1].wait_send)
    for r in range(3):
        for c in range(3):
            wait_send(face_copies(r, c))
    for phase in range(2):
        everything = rows_in.at[phase, pl.ds(0, GROUPS[phase])]
        pltpu.make_async_copy(everything, everything, row_send.at[phase]).wait()


def body(forcing, initial_guess, forward_velocity, free_mask):
    field = (3, 7, 7, 8, 128)
    plane = (7, 7, 8, 128)
    f32 = jnp.float32
    hbm = pl.BlockSpec(memory_space=pltpu.HBM)
    vmem = pl.BlockSpec(memory_space=pltpu.VMEM)
    v1, v2, v3, coef = pl.pallas_call(
        main_kernel,
        out_shape=[jax.ShapeDtypeStruct(field, f32)] * 3
        + [jax.ShapeDtypeStruct((5, 8, 128), f32)],
        in_specs=[hbm] * 5,
        out_specs=[vmem] * 4,
        scratch_shapes=[
            pltpu.VMEM((3, 7, 7, 7, 128), f32),
            pltpu.VMEM((3, 7, 7, 7, 128), f32),
            pltpu.VMEM((3, 7, 7, 7, 128), jnp.bfloat16),
            pltpu.VMEM((7, 7, 7, 128), jnp.int32),
            pltpu.VMEM((NZ * 8 + 2, 8, 128), f32),
            pltpu.VMEM(field, f32),
            pltpu.VMEM(field, f32),
            pltpu.VMEM(plane, f32),
            pltpu.VMEM(field, f32),
            pltpu.VMEM((8, 7, 8, 128), f32),
            pltpu.VMEM((7, 8, 8, 128), f32),
            pltpu.VMEM((8, 7, 8, 128), f32),
            pltpu.VMEM((7, 8, 8, 128), f32),
            pltpu.VMEM((7, 7, NZ, 8, 128), f32),
            pltpu.VMEM(plane, f32),
            pltpu.VMEM(plane, f32),
            pltpu.VMEM((3, 3, 2, 2, 7, 8, 128), f32),
            pltpu.VMEM((3, 3, 2, 7, 8, 128), f32),
            pltpu.VMEM((3, 3, 2, 2, 7, 8, 128), f32),
            pltpu.VMEM((2, 7, 8, 128), f32),
            pltpu.VMEM((2, 1, 128), f32),
            pltpu.VMEM((2, 31, 1, 128), f32),
            pltpu.SemaphoreType.DMA((5,)),
            pltpu.SemaphoreType.DMA((3, 3, 4)),
            pltpu.SemaphoreType.DMA((3, 3, 4)),
            pltpu.SemaphoreType.DMA((4,)),
            pltpu.SemaphoreType.DMA((4,)),
            pltpu.SemaphoreType.DMA((2,)),
            pltpu.SemaphoreType.DMA((2,)),
        ],
        compiler_params=pltpu.CompilerParams(
            collective_id=0, has_side_effects=True, vmem_limit_bytes=32 << 20
        ),
    )(*[pltpu.with_memory_space_constraint(q, pltpu.HBM) for q in (forcing, initial_guess, forward_velocity, free_mask, jnp.asarray(z_constants()))])
    v1, v2, v3 = (v[..., :7, :] for v in (v1, v2, v3))
    coef = coef[:, :3, None, None, None, :]
    guess = initial_guess + coef[0] * v1 + coef[1] * v2
    direction = coef[2] * v1 + coef[3] * v2 + coef[4] * v3
    return guess, direction


def solution(mesh):
    placed = (
        P(None, "px", "py", None, None),
        P(None, "px", "py", None, None),
        P(None, "px", "py", None, None),
        P("px", "py", None, None),
    )
    return jax.shard_map(
        body,
        mesh=mesh,
        in_specs=placed,
        out_specs=(P(None, "px", "py", None, None), P(None, "px", "py", None, None)),
        check_vma=False,
    )
```

```python
import functools

import jax
import jax.numpy as jnp
import numpy as np
from jax import lax
from jax.experimental import pallas as pl
from jax.experimental.pallas import tpu as pltpu
from jax.sharding import PartitionSpec as P

MESH = pl.DeviceIdType.MESH
HELMHOLTZ = 20.0


def gll_tables():
    poly_order = 7
    gll_points = np.array(
        [
            -1.0,
            -0.8717401485096066,
            -0.5917001814331423,
            -0.20929921790247888,
            0.20929921790247888,
            0.5917001814331423,
            0.8717401485096066,
            1.0,
        ]
    )
    previous = np.ones(8)
    legendre = gll_points.copy()
    for degree in range(1, poly_order):
        following = ((2 * degree + 1) * gll_points * legendre - degree * previous) / (degree + 1)
        previous = legendre
        legendre = following
    quad_weights = 2.0 / (poly_order * (poly_order + 1) * legendre**2)
    derivative = np.zeros((8, 8))
    for target in range(8):
        for source in range(8):
            if target != source:
                derivative[target, source] = (
                    legendre[target] / legendre[source] / (gll_points[target] - gll_points[source])
                )
    derivative[0, 0] = -poly_order * (poly_order + 1) / 4.0
    derivative[7, 7] = poly_order * (poly_order + 1) / 4.0
    node_weights = quad_weights[:7].copy()
    node_weights[0] = 2.0 * quad_weights[0]
    return quad_weights, derivative, node_weights


QW, DM, NW = gll_tables()
EVEN = [[float(DM[m, k] + DM[m, 7 - k]) / 2 for k in range(4)] for m in range(4)]
ODD = [[float(DM[m, k] - DM[m, 7 - k]) / 2 for k in range(4)] for m in range(4)]
D77 = float(DM[7, 7])

NZ = 5


def z_constants():
    table = np.zeros((NZ * 8 + 2, 8, 128), np.float32)
    for s in range(NZ):
        for t in range(8):
            for a in range(8):
                m = (a + t) % 8
                table[s * 8 + t, a, :] = DM[m, a] * DM[m, (a + s) % 8]
    for a in range(8):
        table[NZ * 8, a, :] = QW[a]
        table[NZ * 8 + 1, a, :] = NW[a] if a < 7 else 0.0
    return table


def total(terms):
    terms = list(terms)
    while len(terms) > 1:
        terms = [
            terms[i] + terms[i + 1] if i + 1 < len(terms) else terms[i]
            for i in range(0, len(terms), 2)
        ]
    return terms[0]


def by_index(i, table):
    inner = jnp.where((i == 2) | (i == 5), float(table[2]), float(table[3]))
    inner = jnp.where((i == 1) | (i == 6), float(table[1]), inner)
    return jnp.where(i == 0, float(table[0]), inner)


def by_table(i, table):
    value = float(table[6])
    for k in range(5, -1, -1):
        value = jnp.where(i == k, float(table[k]), value)
    return value


def line_apply(v, kappa):
    p = [v[0]] + [v[j] + v[7 - j] for j in range(1, 4)]
    q = [v[0]] + [v[j] - v[7 - j] for j in range(1, 4)]
    a, b = [], []
    for m in range(4):
        even = total(EVEN[m][k] * p[k] for k in range(4))
        odd = total(ODD[m][k] * q[k] for k in range(4))
        first = kappa[m] * (odd + even)
        if 7 - m < len(kappa):
            last = kappa[7 - m] * (odd - even)
            a.append(first - last)
            b.append(first + last)
        else:
            a.append(first)
            b.append(first)
    out = [None] * 8
    for k in range(4):
        r = total(EVEN[m][k] * a[m] for m in range(4))
        t = total(ODD[m][k] * b[m] for m in range(4))
        out[k] = r + t
        if k:
            out[7 - k] = r - t
    return out[:7]


def turned(tile, s):
    return pltpu.roll(tile, 8 - s, 0) if s else tile


def z_apply(closed, diagonals):
    terms = [diagonals[0] * closed, diagonals[4] * turned(closed, 4)]
    for s in range(1, 4):
        terms.append(diagonals[s] * turned(closed, s))
        terms.append(pltpu.roll(diagonals[s] * closed, s, 0))
    return total(terms)


def group(px, py, phase):
    x, y, c = px // 8, lax.rem(px // 2, 4), lax.rem(px, 2)
    if phase == 1:
        offsets = [(0, 0, 0, d) for d in (4, 3, 5, 2, 6, 1, 7)]
    else:
        offsets = [
            (dx, dy, dc, 0)
            for dx in (2, 1, 3, 0)
            for dy in (2, 1, 3, 0)
            for dc in (1, 0)
            if dx or dy or dc
        ]
    out = []
    for dx, dy, dc, dz in offsets:
        nx, ny, nc = lax.rem(x + dx, 4), lax.rem(y + dy, 4), lax.rem(c + dc, 2)
        out.append((nx * 8 + ny * 2 + nc, lax.rem(py + dz, 8)))
    return out


GROUPS = (31, 7)


def main_kernel(
    f_hbm, x_hbm, fv_hbm, m_hbm, z_hbm,
    v1, v2, v3, coef,
    f7, x7, fv7, m7, zc, v0, fm, cv, closing, acc, kx, ky, bx, by, zd, mdi, dg,
    s_out, rv, rs, rb, row_out, rows_in,
    load_sem, send_sem, recv_sem, set_send, set_recv, row_send, row_recv,
):
    px = lax.axis_index("px")
    py = lax.axis_index("py")
    not_first = py > 0
    not_last = py < 7
    prev_x, next_x = (lax.rem(px + 31, 32), py), (lax.rem(px + 1, 32), py)
    prev_y, next_y = (px, lax.rem(py + 7, 8)), (px, lax.rem(py + 1, 8))

    loads = [
        pltpu.make_async_copy(src, dst, load_sem.at[i])
        for i, (src, dst) in enumerate(
            ((fv_hbm, fv7), (x_hbm, x7), (f_hbm, f7), (z_hbm, zc), (m_hbm, m7))
        )
    ]
    for load in loads:
        load.start()

    partners = [group(px, py, phase) for phase in (0, 1)]
    barrier = pltpu.get_barrier_semaphore()
    for device in partners[0] + partners[1]:
        pl.semaphore_signal(barrier, inc=1, device_id=device, device_id_type=MESH)

    zero_row = jnp.zeros((1, 128), jnp.float32)
    zero_face = jnp.zeros((7, 8, 128), jnp.float32)

    @pl.when(py == 0)
    def _():
        rb[1] = zero_face
        for r in range(3):
            for c in range(3):
                rs[r, c, 1, 0] = zero_face
                rs[r, c, 1, 1] = zero_face

    @pl.when(py == 7)
    def _():
        ky[:, 7] = zero_face
        for r in range(3):
            for c in range(3):
                rv[r, c, 1] = zero_face

    rows = lax.broadcasted_iota(jnp.int32, (8, 128), 0)
    lanes = lax.broadcasted_iota(jnp.int32, (8, 128), 1)
    last_row = rows == 7
    each = functools.partial(lax.fori_loop, 0, 7)

    loads[0].wait()

    def viscosity(x, carry):
        for y in range(7):
            speed = [fv7[i, x, y].astype(jnp.float32) for i in range(3)]
            cv[x, y, 0:7, :] = 0.5 + 0.5 * (
                speed[0] * speed[0] + speed[1] * speed[1] + speed[2] * speed[2]
            )
        return carry

    cv[:, :, 7:8, :] = jnp.zeros((7, 7, 1, 128), jnp.float32)
    each(viscosity, 0)
    loads[3].wait()
    nwa = zc[NZ * 8 + 1]

    def coefficients(x, carry):
        wx, nwx = by_index(x, QW), by_index(x, NW)
        for y in range(7):
            base = cv[x, y] * nwa
            kx[x, y] = base * (wx * float(NW[y]))
            ky[x, y] = base * (nwx * float(QW[y]))
        return carry

    each(coefficients, 0)

    def remote(src, dst, send, recv, device):
        return pltpu.make_async_remote_copy(
            src_ref=src,
            dst_ref=dst,
            send_sem=send,
            recv_sem=recv,
            device_id=device,
            device_id_type=MESH,
        )

    setup_copies = [
        remote(kx.at[0], kx.at[7], set_send.at[0], set_recv.at[0], prev_x),
        remote(ky.at[:, 0], ky.at[:, 7], set_send.at[1], set_recv.at[1], prev_y),
        remote(bx.at[7], rb.at[0], set_send.at[2], set_recv.at[2], next_x),
        remote(by.at[:, 7], rb.at[1], set_send.at[3], set_recv.at[3], next_y),
    ]
    vecs = (v0, v1, v2, v3)

    def face_copies(r, c):
        extra = 2 if r == 0 else 1
        v = vecs[r]
        ends = (
            (v.at[c, 0], rv.at[r, c, 0], prev_x),
            (v.at[c, :, 0], rv.at[r, c, 1], prev_y),
            (s_out.at[r, c, 0, 0:extra], rs.at[r, c, 0, 0:extra], next_x),
            (s_out.at[r, c, 1, 0:extra], rs.at[r, c, 1, 0:extra], next_y),
        )
        return [
            remote(src, dst, send_sem.at[r, c, i], recv_sem.at[r, c, i], device)
            for i, (src, dst, device) in enumerate(ends)
        ]

    def start(copies):
        copies[0].start()
        pl.when(not_first)(copies[1].start)
        copies[2].start()
        pl.when(not_last)(copies[3].start)

    def wait_recv(copies):
        copies[0].wait_recv()
        pl.when(not_last)(copies[1].wait_recv)
        copies[2].wait_recv()
        pl.when(not_first)(copies[3].wait_recv)

    def wait_send(copies):
        copies[0].wait_send()
        pl.when(not_first)(copies[1].wait_send)
        copies[2].wait_send()
        pl.when(not_last)(copies[3].wait_send)

    pl.semaphore_wait(barrier, sum(GROUPS))
    setup_copies[0].start()
    pl.when(not_first)(setup_copies[1].start)

    def last_rows(i, carry):
        along_x = [kx[m, i] for m in range(7)]
        for k in range(8):
            bx[k, i] = total(float(DM[m, k] * DM[m, 7]) * along_x[m] for m in range(7))
        along_y = [ky[i, m] for m in range(7)]
        for k in range(8):
            by[i, k] = total(float(DM[m, k] * DM[m, 7]) * along_y[m] for m in range(7))
        return carry

    each(last_rows, 0)
    setup_copies[2].start()
    pl.when(not_last)(setup_copies[3].start)

    loads[1].wait()
    loads[2].wait()

    def spread_inputs(x, carry):
        nwx = by_index(x, NW)
        for c in range(3):
            for y in range(7):
                v0[c, x, y, 0:7, :] = x7[c, x, y]
                v0[c, x, y, 7:8, :] = zero_row
                fm[c, x, y, 0:7, :] = f7[c, x, y] * (nwa[0:7] * (nwx * float(NW[y])))
                fm[c, x, y, 7:8, :] = zero_row
        return carry

    each(spread_inputs, 0)

    for c in range(3):

        def first_sums(i, carry, c=c):
            v = [v0[c, k, i] for k in range(7)]
            s_out[0, c, 0, 0, i] = total(bx[k, i] * v[k] for k in range(7))
            s_out[0, c, 0, 1, i] = total(float(DM[7, k]) * v[k] for k in range(7))
            v = [v0[c, i, k] for k in range(7)]
            s_out[0, c, 1, 0, i] = total(by[i, k] * v[k] for k in range(7))
            s_out[0, c, 1, 1, i] = total(float(DM[7, k]) * v[k] for k in range(7))
            return carry

        each(first_sums, 0)
        start(face_copies(0, c))

    wz = zc[NZ * 8]

    for x in range(7):
        cv[x, :, 7, :] = pltpu.roll(cv[x, :, 0, :], 127, 1)

    def z_setup(x, carry):
        nwx = by_index(x, NW)
        for y in range(7):
            kz = cv[x, y] * (wz * (nwx * float(NW[y])))
            turns = [turned(kz, t) for t in range(8)]
            for s in range(NZ):
                value = total(zc[s * 8 + t] * turns[t] for t in range(8))
                if s == 0:
                    value = value + nwa * (nwx * float(HELMHOLTZ * NW[y]))
                zd[x, y, s] = value
        return carry

    each(z_setup, 0)

    def local_apply(r):
        v_ref = vecs[r]
        points = 8 if r else 7
        for c in range(3):
            for x in range(7):
                closing[c, x] = pltpu.roll(v_ref[c, x, :, 0, :], 127, 1)
        for c in range(3):

            def x_lines(y, carry, c=c):
                out = line_apply(
                    [v_ref[c, k, y] for k in range(7)], [kx[m, y] for m in range(points)]
                )
                for k in range(7):
                    acc[c, k, y] = out[k]
                return carry

            each(x_lines, 0)

            def yz_lines(x, carry, c=c):
                v = [v_ref[c, x, k] for k in range(7)]
                out = line_apply(v, [ky[x, m] for m in range(points)])
                for k in range(7):
                    closed = jnp.where(last_row, closing[c, x, k : k + 1, :], v[k])
                    z_part = z_apply(closed, [zd[x, k, s] for s in range(NZ)])
                    acc[c, x, k] = acc[c, x, k] + out[k] + z_part
                return carry

            each(yz_lines, 0)
        for c in range(3):
            for x in range(7):
                acc[c, x, :, 0, :] = acc[c, x, :, 0, :] + pltpu.roll(acc[c, x, :, 7, :], 1, 1)

    local_apply(0)

    loads[4].wait()
    setup_copies[0].wait_recv()
    pl.when(not_last)(setup_copies[1].wait_recv)
    setup_copies[2].wait_recv()
    pl.when(not_first)(setup_copies[3].wait_recv)
    setup_copies[2].wait_send()
    pl.when(not_last)(setup_copies[3].wait_send)
    inner_y = jnp.where(not_first, D77 * D77, 0.0)

    def first_layers(i, carry):
        layer_x = rb[0, i] + (D77 * D77) * kx[0, i]
        layer_y = rb[1, i] + inner_y * ky[i, 0]
        zd[0, i, 0] = zd[0, i, 0] + layer_x
        zd[i, 0, 0] = zd[i, 0, 0] + layer_y
        for c in range(3):
            acc[c, 0, i] = acc[c, 0, i] + layer_x * v0[c, 0, i]
            acc[c, i, 0] = acc[c, i, 0] + layer_y * v0[c, i, 0]
        return carry

    each(first_layers, 0)

    def x_diagonal(y, carry):
        kappa = [kx[m, y] for m in range(8)]
        for k in range(7):
            dg[k, y] = total(float(DM[m, k] ** 2) * kappa[m] for m in range(8))
            bx[k, y] = bx[k, y] + float(DM[7, k] * D77) * kappa[7]
        return carry

    each(x_diagonal, 0)

    for x in range(7):
        dg[x, :, 0, :] = dg[x, :, 0, :] + pltpu.roll(zd[x, :, 0, 7, :], 1, 1)

    def y_diagonal(x, carry):
        kappa = [ky[x, m] for m in range(8)]
        for k in range(7):
            value = total(float(DM[m, k] ** 2) * kappa[m] for m in range(8))
            by[x, k] = by[x, k] + float(DM[7, k] * D77) * kappa[7]
            value = value + dg[x, k] + zd[x, k, 0]
            dg[x, k] = jnp.where(last_row, 0.0, value)
            mdi[x, k, 0:7, :] = m7[x, k].astype(jnp.float32) / value[0:7]
            mdi[x, k, 7:8, :] = zero_row
        return carry

    each(y_diagonal, 0)

    zero_tile = jnp.zeros((8, 128), jnp.float32)
    moments = {}

    def finish(r, c):
        v_ref, u_ref = vecs[r], vecs[r + 1]
        for i in range(7):
            sum_x, sum_y = rs[r, c, 0, 0, i], rs[r, c, 1, 0, i]
            if r == 0:
                sum_x = sum_x + D77 * kx[0, i] * rs[r, c, 0, 1, i]
                sum_y = sum_y + D77 * ky[i, 0] * rs[r, c, 1, 1, i]
            acc[c, 0, i] = acc[c, 0, i] + sum_x
            acc[c, i, 0] = acc[c, i, 0] + sum_y

        def row(x, carry):
            sums, tally = carry
            sums, tally = list(sums), list(tally)
            end_y = rv[r, c, 1, x]
            sum_y = []
            if r == 0:
                at_end = by_table(x, DM[7])
                last_y = ky[x, 7] * s_out[0, c, 1, 1, x]
            for y in range(7):
                b_x, b_y = bx[x, y], by[x, y]
                t = acc[c, x, y] + b_x * rv[r, c, 0, y] + b_y * end_y
                if r == 0:
                    t = t + at_end * (kx[7, y] * s_out[0, c, 0, 1, y]) + float(DM[7, y]) * last_y
                    u = mdi[x, y] * (fm[c, x, y] - t)
                else:
                    v = v_ref[c, x, y]
                    u = v - mdi[x, y] * t
                u_ref[c, x, y] = u
                if r < 2:
                    sums[y] = sums[y] + b_x * u
                    sum_y.append(b_y * u)
                weighted = dg[x, y] * u
                if r:
                    tally[0] = tally[0] + v * weighted
                tally[1] = tally[1] + u * weighted
            if r < 2:
                s_out[r + 1, c, 1, 0, x] = total(sum_y)
            return tuple(sums), tuple(tally)

        sums, tally = each(row, ((zero_tile,) * (7 if r < 2 else 0), (zero_tile,) * 2))
        if r < 2:
            for y in range(7):
                s_out[r + 1, c, 0, 0, y] = sums[y]
        if r:
            moments[2 * r - 1, c] = tally[0]
        moments[2 * r, c] = tally[1]

    for r in range(3):
        if r:
            local_apply(r)
        for c in range(3):
            wait_recv(face_copies(r, c))
            finish(r, c)
            if r < 2:
                start(face_copies(r + 1, c))

    halves = []
    for half in range(2):
        stack = zero_tile
        for j in range(8):
            index = half * 8 + j
            if index < 15:
                value = jnp.sum(moments[index // 3, index % 3], axis=0, keepdims=True)
                stack = jnp.where(rows == j, value, stack)
        value = jnp.sum(stack, axis=1, keepdims=True)
        halves.append(jnp.where(lanes == rows + 8 * half, value, 0.0))
    row_total = jnp.sum(halves[0] + halves[1], axis=0, keepdims=True)

    for phase in range(2):
        count = GROUPS[phase]
        row_out[phase] = row_total
        for slot, device in enumerate(partners[phase]):
            remote(
                row_out.at[phase],
                rows_in.at[phase, slot],
                row_send.at[phase],
                row_recv.at[phase],
                device,
            ).start()
        everything = rows_in.at[phase, pl.ds(0, count)]
        pltpu.make_async_copy(everything, everything, row_recv.at[phase]).wait()
        row_total = total([row_total] + [rows_in[phase, slot] for slot in range(count)])

    n = []
    for k in range(5):
        picked = jnp.where(lanes == rows + 3 * k, jnp.broadcast_to(row_total, (8, 128)), 0.0)
        n.append(jnp.broadcast_to(jnp.sum(picked, axis=1, keepdims=True), (8, 128)))
    alpha0 = n[0] / (n[0] - n[1])
    a = -n[1] / (n[0] - n[1])
    e1 = a * a * n[0] + 2.0 * a * alpha0 * n[1] + alpha0 * alpha0 * n[2]
    b = a + e1 / n[0]
    curvature = (
        b * b * (n[0] - n[1]) + 2.0 * b * alpha0 * (n[1] - n[2]) + alpha0 * alpha0 * (n[2] - n[3])
    )
    alpha1 = e1 / curvature
    a0 = a - alpha1 * b
    a1 = alpha0 - alpha1 * (alpha0 - b)
    a2 = alpha1 * alpha0
    e2 = (
        a0 * a0 * n[0]
        + 2.0 * a0 * a1 * n[1]
        + (a1 * a1 + 2.0 * a0 * a2) * n[2]
        + 2.0 * a1 * a2 * n[3]
        + a2 * a2 * n[4]
    )
    beta1 = e2 / e1
    coef[0] = alpha0 + alpha1 * b
    coef[1] = a2
    coef[2] = a0 + beta1 * b
    coef[3] = a1 + beta1 * alpha0
    coef[4] = a2

    setup_copies[0].wait_send()
    pl.when(not_first)(setup_copies[1].wait_send)
    for r in range(3):
        for c in range(3):
            wait_send(face_copies(r, c))
    for phase in range(2):
        everything = rows_in.at[phase, pl.ds(0, GROUPS[phase])]
        pltpu.make_async_copy(everything, everything, row_send.at[phase]).wait()


def body(forcing, initial_guess, forward_velocity, free_mask):
    field = (3, 7, 7, 8, 128)
    plane = (7, 7, 8, 128)
    f32 = jnp.float32
    hbm = pl.BlockSpec(memory_space=pltpu.HBM)
    vmem = pl.BlockSpec(memory_space=pltpu.VMEM)
    v1, v2, v3, coef = pl.pallas_call(
        main_kernel,
        out_shape=[jax.ShapeDtypeStruct(field, f32)] * 3
        + [jax.ShapeDtypeStruct((5, 8, 128), f32)],
        in_specs=[hbm] * 5,
        out_specs=[vmem] * 4,
        scratch_shapes=[
            pltpu.VMEM((3, 7, 7, 7, 128), f32),
            pltpu.VMEM((3, 7, 7, 7, 128), f32),
            pltpu.VMEM((3, 7, 7, 7, 128), jnp.bfloat16),
            pltpu.VMEM((7, 7, 7, 128), jnp.int32),
            pltpu.VMEM((NZ * 8 + 2, 8, 128), f32),
            pltpu.VMEM(field, f32),
            pltpu.VMEM(field, f32),
            pltpu.VMEM(plane, f32),
            pltpu.VMEM((3, 7, 7, 128), f32),
            pltpu.VMEM(field, f32),
            pltpu.VMEM((8, 7, 8, 128), f32),
            pltpu.VMEM((7, 8, 8, 128), f32),
            pltpu.VMEM((8, 7, 8, 128), f32),
            pltpu.VMEM((7, 8, 8, 128), f32),
            pltpu.VMEM((7, 7, NZ, 8, 128), f32),
            pltpu.VMEM(plane, f32),
            pltpu.VMEM(plane, f32),
            pltpu.VMEM((3, 3, 2, 2, 7, 8, 128), f32),
            pltpu.VMEM((3, 3, 2, 7, 8, 128), f32),
            pltpu.VMEM((3, 3, 2, 2, 7, 8, 128), f32),
            pltpu.VMEM((2, 7, 8, 128), f32),
            pltpu.VMEM((2, 1, 128), f32),
            pltpu.VMEM((2, 31, 1, 128), f32),
            pltpu.SemaphoreType.DMA((5,)),
            pltpu.SemaphoreType.DMA((3, 3, 4)),
            pltpu.SemaphoreType.DMA((3, 3, 4)),
            pltpu.SemaphoreType.DMA((4,)),
            pltpu.SemaphoreType.DMA((4,)),
            pltpu.SemaphoreType.DMA((2,)),
            pltpu.SemaphoreType.DMA((2,)),
        ],
        compiler_params=pltpu.CompilerParams(
            collective_id=0, has_side_effects=True, vmem_limit_bytes=32 << 20
        ),
    )(*[pltpu.with_memory_space_constraint(q, pltpu.HBM) for q in (forcing, initial_guess, forward_velocity, free_mask, jnp.asarray(z_constants()))])
    v1, v2, v3 = (v[..., :7, :] for v in (v1, v2, v3))
    coef = coef[:, :3, None, None, None, :]
    guess = initial_guess + coef[0] * v1 + coef[1] * v2
    direction = coef[2] * v1 + coef[3] * v2 + coef[4] * v3
    return guess, direction


def solution(mesh):
    placed = (
        P(None, "px", "py", None, None),
        P(None, "px", "py", None, None),
        P(None, "px", "py", None, None),
        P("px", "py", None, None),
    )
    return jax.shard_map(
        body,
        mesh=mesh,
        in_specs=placed,
        out_specs=(P(None, "px", "py", None, None), P(None, "px", "py", None, None)),
        check_vma=False,
    )
```

```python
import functools

import jax
import jax.numpy as jnp
import numpy as np
from jax import lax
from jax.experimental import pallas as pl
from jax.experimental.pallas import tpu as pltpu
from jax.sharding import PartitionSpec as P

MESH = pl.DeviceIdType.MESH
HELMHOLTZ = 20.0


def gll_tables():
    poly_order = 7
    gll_points = np.array(
        [
            -1.0,
            -0.8717401485096066,
            -0.5917001814331423,
            -0.20929921790247888,
            0.20929921790247888,
            0.5917001814331423,
            0.8717401485096066,
            1.0,
        ]
    )
    previous = np.ones(8)
    legendre = gll_points.copy()
    for degree in range(1, poly_order):
        following = ((2 * degree + 1) * gll_points * legendre - degree * previous) / (degree + 1)
        previous = legendre
        legendre = following
    quad_weights = 2.0 / (poly_order * (poly_order + 1) * legendre**2)
    derivative = np.zeros((8, 8))
    for target in range(8):
        for source in range(8):
            if target != source:
                derivative[target, source] = (
                    legendre[target] / legendre[source] / (gll_points[target] - gll_points[source])
                )
    derivative[0, 0] = -poly_order * (poly_order + 1) / 4.0
    derivative[7, 7] = poly_order * (poly_order + 1) / 4.0
    node_weights = quad_weights[:7].copy()
    node_weights[0] = 2.0 * quad_weights[0]
    return quad_weights, derivative, node_weights


QW, DM, NW = gll_tables()
EVEN = [[float(DM[m, k] + DM[m, 7 - k]) / 2 for k in range(4)] for m in range(4)]
ODD = [[float(DM[m, k] - DM[m, 7 - k]) / 2 for k in range(4)] for m in range(4)]
D77 = float(DM[7, 7])

NZ = 5


def z_constants():
    table = np.zeros((NZ * 8 + 2, 8, 128), np.float32)
    for s in range(NZ):
        for t in range(8):
            for a in range(8):
                m = (a + t) % 8
                table[s * 8 + t, a, :] = DM[m, a] * DM[m, (a + s) % 8]
    for a in range(8):
        table[NZ * 8, a, :] = QW[a]
        table[NZ * 8 + 1, a, :] = NW[a] if a < 7 else 0.0
    return table


def total(terms):
    terms = list(terms)
    while len(terms) > 1:
        terms = [
            terms[i] + terms[i + 1] if i + 1 < len(terms) else terms[i]
            for i in range(0, len(terms), 2)
        ]
    return terms[0]


def by_index(i, table):
    inner = jnp.where((i == 2) | (i == 5), float(table[2]), float(table[3]))
    inner = jnp.where((i == 1) | (i == 6), float(table[1]), inner)
    return jnp.where(i == 0, float(table[0]), inner)


def by_table(i, table):
    value = float(table[6])
    for k in range(5, -1, -1):
        value = jnp.where(i == k, float(table[k]), value)
    return value


def line_apply(v, kappa):
    p = [v[0]] + [v[j] + v[7 - j] for j in range(1, 4)]
    q = [v[0]] + [v[j] - v[7 - j] for j in range(1, 4)]
    a, b = [], []
    for m in range(4):
        even = total(EVEN[m][k] * p[k] for k in range(4))
        odd = total(ODD[m][k] * q[k] for k in range(4))
        first = kappa[m] * (odd + even)
        if 7 - m < len(kappa):
            last = kappa[7 - m] * (odd - even)
            a.append(first - last)
            b.append(first + last)
        else:
            a.append(first)
            b.append(first)
    out = [None] * 8
    for k in range(4):
        r = total(EVEN[m][k] * a[m] for m in range(4))
        t = total(ODD[m][k] * b[m] for m in range(4))
        out[k] = r + t
        if k:
            out[7 - k] = r - t
    return out[:7]


def turned(tile, s):
    return pltpu.roll(tile, 8 - s, 0) if s else tile


def z_apply(closed, diagonals):
    terms = [diagonals[0] * closed, diagonals[4] * turned(closed, 4)]
    for s in range(1, 4):
        terms.append(diagonals[s] * turned(closed, s))
        terms.append(pltpu.roll(diagonals[s] * closed, s, 0))
    return total(terms)


CHIPS = 128
Z_ORDER = (4, 3, 5, 2, 6, 1, 7, 0)
GREETINGS = (("z", 1), ("z", 2), ("x", 1), ("x", 1), ("y", 1), ("y", 1))


def main_kernel(
    f_hbm, x_hbm, fv_hbm, m_hbm, z_hbm,
    v1, v2, v3, coef,
    f7, x7, fv7, m7, zc, v0, fm, cv, closing, acc, kx, ky, bx, by, zd, mdi, dg,
    s_out, rv, rs, rb, row_out, rows_in,
    load_sem, send_sem, recv_sem, set_send, set_recv, row_send, row_recv, greet_sem,
):
    px = lax.axis_index("px")
    py = lax.axis_index("py")
    not_first = py > 0
    not_last = py < 7
    prev_x, next_x = (lax.rem(px + 31, 32), py), (lax.rem(px + 1, 32), py)
    prev_y, next_y = (px, lax.rem(py + 7, 8)), (px, lax.rem(py + 1, 8))

    loads = [
        pltpu.make_async_copy(src, dst, load_sem.at[i])
        for i, (src, dst) in enumerate(
            ((fv_hbm, fv7), (x_hbm, x7), (f_hbm, f7), (z_hbm, zc), (m_hbm, m7))
        )
    ]
    for load in loads:
        load.start()

    at = {"x": px // 8, "y": lax.rem(px // 2, 4), "z": py}
    core = lax.rem(px, 2)
    other_core = (px + 1 - 2 * core, py)

    def chip(x=0, y=0, z=0):
        nx, ny, nz = lax.rem(at["x"] + x, 4), lax.rem(at["y"] + y, 4), lax.rem(at["z"] + z, 8)
        return (nx * 8 + ny * 2 + core, nz)

    def around(axis, distance):
        return chip(**{axis: distance}), chip(**{axis: (8 if axis == "z" else 4) - distance})

    barrier = pltpu.get_barrier_semaphore()
    greeted = (*around("y", 1), *around("x", 1), *around("z", 1), prev_x, next_x)
    for device in greeted:
        pl.semaphore_signal(barrier, inc=1, device_id=device, device_id_type=MESH)

    def greet(step):
        if step:
            pl.semaphore_wait(greet_sem.at[step - 1], 2)
        if step < len(GREETINGS):
            for device in around(*GREETINGS[step]):
                pl.semaphore_signal(
                    greet_sem.at[step], inc=1, device_id=device, device_id_type=MESH
                )

    zero_row = jnp.zeros((1, 128), jnp.float32)
    zero_face = jnp.zeros((7, 8, 128), jnp.float32)

    @pl.when(py == 0)
    def _():
        rb[1] = zero_face
        for r in range(3):
            for c in range(3):
                rs[r, c, 1, 0] = zero_face
                rs[r, c, 1, 1] = zero_face

    @pl.when(py == 7)
    def _():
        ky[:, 7] = zero_face
        for r in range(3):
            for c in range(3):
                rv[r, c, 1] = zero_face

    rows = lax.broadcasted_iota(jnp.int32, (8, 128), 0)
    lanes = lax.broadcasted_iota(jnp.int32, (8, 128), 1)
    last_row = rows == 7
    each = functools.partial(lax.fori_loop, 0, 7)

    loads[0].wait()

    def viscosity(x, carry):
        for y in range(7):
            speed = [fv7[i, x, y].astype(jnp.float32) for i in range(3)]
            cv[x, y, 0:7, :] = 0.5 + 0.5 * (
                speed[0] * speed[0] + speed[1] * speed[1] + speed[2] * speed[2]
            )
        return carry

    cv[:, :, 7:8, :] = jnp.zeros((7, 7, 1, 128), jnp.float32)
    each(viscosity, 0)
    loads[3].wait()
    nwa = zc[NZ * 8 + 1]

    def coefficients(x, carry):
        wx, nwx = by_index(x, QW), by_index(x, NW)
        for y in range(7):
            base = cv[x, y] * nwa
            kx[x, y] = base * (wx * float(NW[y]))
            ky[x, y] = base * (nwx * float(QW[y]))
        return carry

    each(coefficients, 0)

    def remote(src, dst, send, recv, device):
        return pltpu.make_async_remote_copy(
            src_ref=src,
            dst_ref=dst,
            send_sem=send,
            recv_sem=recv,
            device_id=device,
            device_id_type=MESH,
        )

    setup_copies = [
        remote(kx.at[0], kx.at[7], set_send.at[0], set_recv.at[0], prev_x),
        remote(ky.at[:, 0], ky.at[:, 7], set_send.at[1], set_recv.at[1], prev_y),
        remote(bx.at[7], rb.at[0], set_send.at[2], set_recv.at[2], next_x),
        remote(by.at[:, 7], rb.at[1], set_send.at[3], set_recv.at[3], next_y),
    ]
    vecs = (v0, v1, v2, v3)

    def face_copies(r, c):
        extra = 2 if r == 0 else 1
        v = vecs[r]
        ends = (
            (v.at[c, 0], rv.at[r, c, 0], prev_x),
            (v.at[c, :, 0], rv.at[r, c, 1], prev_y),
            (s_out.at[r, c, 0, 0:extra], rs.at[r, c, 0, 0:extra], next_x),
            (s_out.at[r, c, 1, 0:extra], rs.at[r, c, 1, 0:extra], next_y),
        )
        return [
            remote(src, dst, send_sem.at[r, c, i], recv_sem.at[r, c, i], device)
            for i, (src, dst, device) in enumerate(ends)
        ]

    def start(copies):
        copies[0].start()
        pl.when(not_first)(copies[1].start)
        copies[2].start()
        pl.when(not_last)(copies[3].start)

    def wait_recv(copies):
        copies[0].wait_recv()
        pl.when(not_last)(copies[1].wait_recv)
        copies[2].wait_recv()
        pl.when(not_first)(copies[3].wait_recv)

    def wait_send(copies):
        copies[0].wait_send()
        pl.when(not_first)(copies[1].wait_send)
        copies[2].wait_send()
        pl.when(not_last)(copies[3].wait_send)

    pl.semaphore_wait(barrier, len(greeted))
    setup_copies[0].start()
    pl.when(not_first)(setup_copies[1].start)
    greet(0)

    def last_rows(i, carry):
        along_x = [kx[m, i] for m in range(7)]
        for k in range(8):
            bx[k, i] = total(float(DM[m, k] * DM[m, 7]) * along_x[m] for m in range(7))
        along_y = [ky[i, m] for m in range(7)]
        for k in range(8):
            by[i, k] = total(float(DM[m, k] * DM[m, 7]) * along_y[m] for m in range(7))
        return carry

    each(last_rows, 0)
    setup_copies[2].start()
    pl.when(not_last)(setup_copies[3].start)

    loads[1].wait()
    loads[2].wait()

    def spread_inputs(x, carry):
        nwx = by_index(x, NW)
        for c in range(3):
            for y in range(7):
                v0[c, x, y, 0:7, :] = x7[c, x, y]
                v0[c, x, y, 7:8, :] = zero_row
                fm[c, x, y, 0:7, :] = f7[c, x, y] * (nwa[0:7] * (nwx * float(NW[y])))
                fm[c, x, y, 7:8, :] = zero_row
        return carry

    each(spread_inputs, 0)

    for c in range(3):

        def first_sums(i, carry, c=c):
            v = [v0[c, k, i] for k in range(7)]
            s_out[0, c, 0, 0, i] = total(bx[k, i] * v[k] for k in range(7))
            s_out[0, c, 0, 1, i] = total(float(DM[7, k]) * v[k] for k in range(7))
            v = [v0[c, i, k] for k in range(7)]
            s_out[0, c, 1, 0, i] = total(by[i, k] * v[k] for k in range(7))
            s_out[0, c, 1, 1, i] = total(float(DM[7, k]) * v[k] for k in range(7))
            return carry

        each(first_sums, 0)
        start(face_copies(0, c))

    greet(1)

    wz = zc[NZ * 8]

    for x in range(7):
        cv[x, :, 7, :] = pltpu.roll(cv[x, :, 0, :], 127, 1)

    def z_setup(x, carry):
        nwx = by_index(x, NW)
        for y in range(7):
            kz = cv[x, y] * (wz * (nwx * float(NW[y])))
            turns = [turned(kz, t) for t in range(8)]
            for s in range(NZ):
                value = total(zc[s * 8 + t] * turns[t] for t in range(8))
                if s == 0:
                    value = value + nwa * (nwx * float(HELMHOLTZ * NW[y]))
                zd[x, y, s] = value
        return carry

    each(z_setup, 0)
    greet(2)

    def local_apply(r):
        v_ref = vecs[r]
        points = 8 if r else 7
        for c in range(3):
            for x in range(7):
                closing[c, x] = pltpu.roll(v_ref[c, x, :, 0, :], 127, 1)
        for c in range(3):

            def x_lines(y, carry, c=c):
                out = line_apply(
                    [v_ref[c, k, y] for k in range(7)], [kx[m, y] for m in range(points)]
                )
                for k in range(7):
                    acc[c, k, y] = out[k]
                return carry

            each(x_lines, 0)

            def yz_lines(x, carry, c=c):
                v = [v_ref[c, x, k] for k in range(7)]
                out = line_apply(v, [ky[x, m] for m in range(points)])
                for k in range(7):
                    closed = jnp.where(last_row, closing[c, x, k : k + 1, :], v[k])
                    z_part = z_apply(closed, [zd[x, k, s] for s in range(NZ)])
                    acc[c, x, k] = acc[c, x, k] + out[k] + z_part
                return carry

            each(yz_lines, 0)
        for c in range(3):
            for x in range(7):
                acc[c, x, :, 0, :] = acc[c, x, :, 0, :] + pltpu.roll(acc[c, x, :, 7, :], 1, 1)

    local_apply(0)
    greet(3)

    loads[4].wait()
    setup_copies[0].wait_recv()
    pl.when(not_last)(setup_copies[1].wait_recv)
    setup_copies[2].wait_recv()
    pl.when(not_first)(setup_copies[3].wait_recv)
    setup_copies[2].wait_send()
    pl.when(not_last)(setup_copies[3].wait_send)
    inner_y = jnp.where(not_first, D77 * D77, 0.0)

    def first_layers(i, carry):
        layer_x = rb[0, i] + (D77 * D77) * kx[0, i]
        layer_y = rb[1, i] + inner_y * ky[i, 0]
        zd[0, i, 0] = zd[0, i, 0] + layer_x
        zd[i, 0, 0] = zd[i, 0, 0] + layer_y
        for c in range(3):
            acc[c, 0, i] = acc[c, 0, i] + layer_x * v0[c, 0, i]
            acc[c, i, 0] = acc[c, i, 0] + layer_y * v0[c, i, 0]
        return carry

    each(first_layers, 0)

    def x_diagonal(y, carry):
        kappa = [kx[m, y] for m in range(8)]
        for k in range(7):
            dg[k, y] = total(float(DM[m, k] ** 2) * kappa[m] for m in range(8))
            bx[k, y] = bx[k, y] + float(DM[7, k] * D77) * kappa[7]
        return carry

    each(x_diagonal, 0)

    for x in range(7):
        dg[x, :, 0, :] = dg[x, :, 0, :] + pltpu.roll(zd[x, :, 0, 7, :], 1, 1)

    def y_diagonal(x, carry):
        kappa = [ky[x, m] for m in range(8)]
        for k in range(7):
            value = total(float(DM[m, k] ** 2) * kappa[m] for m in range(8))
            by[x, k] = by[x, k] + float(DM[7, k] * D77) * kappa[7]
            value = value + dg[x, k] + zd[x, k, 0]
            dg[x, k] = jnp.where(last_row, 0.0, value)
            mdi[x, k, 0:7, :] = m7[x, k].astype(jnp.float32) / value[0:7]
            mdi[x, k, 7:8, :] = zero_row
        return carry

    each(y_diagonal, 0)

    zero_tile = jnp.zeros((8, 128), jnp.float32)
    moments = {}

    def finish(r, c):
        v_ref, u_ref = vecs[r], vecs[r + 1]
        for i in range(7):
            sum_x, sum_y = rs[r, c, 0, 0, i], rs[r, c, 1, 0, i]
            if r == 0:
                sum_x = sum_x + D77 * kx[0, i] * rs[r, c, 0, 1, i]
                sum_y = sum_y + D77 * ky[i, 0] * rs[r, c, 1, 1, i]
            acc[c, 0, i] = acc[c, 0, i] + sum_x
            acc[c, i, 0] = acc[c, i, 0] + sum_y

        def row(x, carry):
            sums, tally = carry
            sums, tally = list(sums), list(tally)
            end_y = rv[r, c, 1, x]
            sum_y = []
            if r == 0:
                at_end = by_table(x, DM[7])
                last_y = ky[x, 7] * s_out[0, c, 1, 1, x]
            for y in range(7):
                b_x, b_y = bx[x, y], by[x, y]
                t = acc[c, x, y] + b_x * rv[r, c, 0, y] + b_y * end_y
                if r == 0:
                    t = t + at_end * (kx[7, y] * s_out[0, c, 0, 1, y]) + float(DM[7, y]) * last_y
                    u = mdi[x, y] * (fm[c, x, y] - t)
                else:
                    v = v_ref[c, x, y]
                    u = v - mdi[x, y] * t
                u_ref[c, x, y] = u
                if r < 2:
                    sums[y] = sums[y] + b_x * u
                    sum_y.append(b_y * u)
                weighted = dg[x, y] * u
                if r:
                    tally[0] = tally[0] + v * weighted
                tally[1] = tally[1] + u * weighted
            if r < 2:
                s_out[r + 1, c, 1, 0, x] = total(sum_y)
            return tuple(sums), tuple(tally)

        sums, tally = each(row, ((zero_tile,) * (7 if r < 2 else 0), (zero_tile,) * 2))
        if r < 2:
            for y in range(7):
                s_out[r + 1, c, 0, 0, y] = sums[y]
        if r:
            moments[2 * r - 1, c] = tally[0]
        moments[2 * r, c] = tally[1]

    for r in range(3):
        if r:
            local_apply(r)
            greet(4 + r)
        for c in range(3):
            wait_recv(face_copies(r, c))
            finish(r, c)
            if r < 2:
                start(face_copies(r + 1, c))
        if r == 0:
            greet(4)

    halves = []
    for half in range(2):
        stack = zero_tile
        for j in range(8):
            index = half * 8 + j
            if index < 15:
                value = jnp.sum(moments[index // 3, index % 3], axis=0, keepdims=True)
                stack = jnp.where(rows == j, value, stack)
        value = jnp.sum(stack, axis=1, keepdims=True)
        halves.append(jnp.where(lanes == rows + 8 * half, value, 0.0))
    row_total = jnp.sum(halves[0] + halves[1], axis=0, keepdims=True)

    row_out[0] = row_total
    pair = remote(row_out.at[0], rows_in.at[CHIPS - 1], row_send.at[0], row_recv.at[0], other_core)
    pair.start()
    pair.wait_recv()
    row_total = row_total + rows_in[CHIPS - 1]
    row_out[1] = row_total
    for place, dz in enumerate(Z_ORDER):

        def send(i, carry, place=place, dz=dz):
            remote(
                row_out.at[1],
                rows_in.at[16 * place + i],
                row_send.at[1],
                row_recv.at[1],
                chip(3 - i // 4, 3 - lax.rem(i, 4), dz),
            ).start()
            return carry

        lax.fori_loop(0, 16 if dz else 15, send, 0)
    everything = rows_in.at[pl.ds(0, CHIPS - 1)]
    pltpu.make_async_copy(everything, everything, row_recv.at[1]).wait()
    row_total = total([row_total] + [rows_in[slot] for slot in range(CHIPS - 1)])

    n = []
    for k in range(5):
        picked = jnp.where(lanes == rows + 3 * k, jnp.broadcast_to(row_total, (8, 128)), 0.0)
        n.append(jnp.broadcast_to(jnp.sum(picked, axis=1, keepdims=True), (8, 128)))
    alpha0 = n[0] / (n[0] - n[1])
    a = -n[1] / (n[0] - n[1])
    e1 = a * a * n[0] + 2.0 * a * alpha0 * n[1] + alpha0 * alpha0 * n[2]
    b = a + e1 / n[0]
    curvature = (
        b * b * (n[0] - n[1]) + 2.0 * b * alpha0 * (n[1] - n[2]) + alpha0 * alpha0 * (n[2] - n[3])
    )
    alpha1 = e1 / curvature
    a0 = a - alpha1 * b
    a1 = alpha0 - alpha1 * (alpha0 - b)
    a2 = alpha1 * alpha0
    e2 = (
        a0 * a0 * n[0]
        + 2.0 * a0 * a1 * n[1]
        + (a1 * a1 + 2.0 * a0 * a2) * n[2]
        + 2.0 * a1 * a2 * n[3]
        + a2 * a2 * n[4]
    )
    beta1 = e2 / e1
    coef[0] = alpha0 + alpha1 * b
    coef[1] = a2
    coef[2] = a0 + beta1 * b
    coef[3] = a1 + beta1 * alpha0
    coef[4] = a2

    setup_copies[0].wait_send()
    pl.when(not_first)(setup_copies[1].wait_send)
    for r in range(3):
        for c in range(3):
            wait_send(face_copies(r, c))
    pair.wait_send()
    pltpu.make_async_copy(everything, everything, row_send.at[1]).wait()


def body(forcing, initial_guess, forward_velocity, free_mask):
    field = (3, 7, 7, 8, 128)
    plane = (7, 7, 8, 128)
    f32 = jnp.float32
    hbm = pl.BlockSpec(memory_space=pltpu.HBM)
    vmem = pl.BlockSpec(memory_space=pltpu.VMEM)
    v1, v2, v3, coef = pl.pallas_call(
        main_kernel,
        out_shape=[jax.ShapeDtypeStruct(field, f32)] * 3
        + [jax.ShapeDtypeStruct((5, 8, 128), f32)],
        in_specs=[hbm] * 5,
        out_specs=[vmem] * 4,
        scratch_shapes=[
            pltpu.VMEM((3, 7, 7, 7, 128), f32),
            pltpu.VMEM((3, 7, 7, 7, 128), f32),
            pltpu.VMEM((3, 7, 7, 7, 128), jnp.bfloat16),
            pltpu.VMEM((7, 7, 7, 128), jnp.int32),
            pltpu.VMEM((NZ * 8 + 2, 8, 128), f32),
            pltpu.VMEM(field, f32),
            pltpu.VMEM(field, f32),
            pltpu.VMEM(plane, f32),
            pltpu.VMEM((3, 7, 7, 128), f32),
            pltpu.VMEM(field, f32),
            pltpu.VMEM((8, 7, 8, 128), f32),
            pltpu.VMEM((7, 8, 8, 128), f32),
            pltpu.VMEM((8, 7, 8, 128), f32),
            pltpu.VMEM((7, 8, 8, 128), f32),
            pltpu.VMEM((7, 7, NZ, 8, 128), f32),
            pltpu.VMEM(plane, f32),
            pltpu.VMEM(plane, f32),
            pltpu.VMEM((3, 3, 2, 2, 7, 8, 128), f32),
            pltpu.VMEM((3, 3, 2, 7, 8, 128), f32),
            pltpu.VMEM((3, 3, 2, 2, 7, 8, 128), f32),
            pltpu.VMEM((2, 7, 8, 128), f32),
            pltpu.VMEM((2, 1, 128), f32),
            pltpu.VMEM((CHIPS, 1, 128), f32),
            pltpu.SemaphoreType.DMA((5,)),
            pltpu.SemaphoreType.DMA((3, 3, 4)),
            pltpu.SemaphoreType.DMA((3, 3, 4)),
            pltpu.SemaphoreType.DMA((4,)),
            pltpu.SemaphoreType.DMA((4,)),
            pltpu.SemaphoreType.DMA((2,)),
            pltpu.SemaphoreType.DMA((2,)),
            pltpu.SemaphoreType.REGULAR((len(GREETINGS),)),
        ],
        compiler_params=pltpu.CompilerParams(
            collective_id=0, has_side_effects=True, vmem_limit_bytes=32 << 20
        ),
    )(*[pltpu.with_memory_space_constraint(q, pltpu.HBM) for q in (forcing, initial_guess, forward_velocity, free_mask, jnp.asarray(z_constants()))])
    v1, v2, v3 = (v[..., :7, :] for v in (v1, v2, v3))
    coef = coef[:, :3, None, None, None, :]
    guess = initial_guess + coef[0] * v1 + coef[1] * v2
    direction = coef[2] * v1 + coef[3] * v2 + coef[4] * v3
    return guess, direction


def solution(mesh):
    placed = (
        P(None, "px", "py", None, None),
        P(None, "px", "py", None, None),
        P(None, "px", "py", None, None),
        P("px", "py", None, None),
    )
    return jax.shard_map(
        body,
        mesh=mesh,
        in_specs=placed,
        out_specs=(P(None, "px", "py", None, None), P(None, "px", "py", None, None)),
        check_vma=False,
    )
```

```python
import functools

import jax
import jax.numpy as jnp
import numpy as np
from jax import lax
from jax.experimental import pallas as pl
from jax.experimental.pallas import tpu as pltpu
from jax.sharding import PartitionSpec as P

MESH = pl.DeviceIdType.MESH
HELMHOLTZ = 20.0


def gll_tables():
    poly_order = 7
    gll_points = np.array(
        [
            -1.0,
            -0.8717401485096066,
            -0.5917001814331423,
            -0.20929921790247888,
            0.20929921790247888,
            0.5917001814331423,
            0.8717401485096066,
            1.0,
        ]
    )
    previous = np.ones(8)
    legendre = gll_points.copy()
    for degree in range(1, poly_order):
        following = ((2 * degree + 1) * gll_points * legendre - degree * previous) / (degree + 1)
        previous = legendre
        legendre = following
    quad_weights = 2.0 / (poly_order * (poly_order + 1) * legendre**2)
    derivative = np.zeros((8, 8))
    for target in range(8):
        for source in range(8):
            if target != source:
                derivative[target, source] = (
                    legendre[target] / legendre[source] / (gll_points[target] - gll_points[source])
                )
    derivative[0, 0] = -poly_order * (poly_order + 1) / 4.0
    derivative[7, 7] = poly_order * (poly_order + 1) / 4.0
    node_weights = quad_weights[:7].copy()
    node_weights[0] = 2.0 * quad_weights[0]
    return quad_weights, derivative, node_weights


QW, DM, NW = gll_tables()
EVEN = [[float(DM[m, k] + DM[m, 7 - k]) / 2 for k in range(4)] for m in range(4)]
ODD = [[float(DM[m, k] - DM[m, 7 - k]) / 2 for k in range(4)] for m in range(4)]
D77 = float(DM[7, 7])

NZ = 5


def z_constants():
    table = np.zeros((NZ * 8 + 2, 8, 128), np.float32)
    for s in range(NZ):
        for t in range(8):
            for a in range(8):
                m = (a + t) % 8
                table[s * 8 + t, a, :] = DM[m, a] * DM[m, (a + s) % 8]
    for a in range(8):
        table[NZ * 8, a, :] = QW[a]
        table[NZ * 8 + 1, a, :] = NW[a] if a < 7 else 0.0
    return table


def total(terms):
    terms = list(terms)
    while len(terms) > 1:
        terms = [
            terms[i] + terms[i + 1] if i + 1 < len(terms) else terms[i]
            for i in range(0, len(terms), 2)
        ]
    return terms[0]


def by_index(i, table):
    inner = jnp.where((i == 2) | (i == 5), float(table[2]), float(table[3]))
    inner = jnp.where((i == 1) | (i == 6), float(table[1]), inner)
    return jnp.where(i == 0, float(table[0]), inner)


def by_table(i, table):
    value = float(table[6])
    for k in range(5, -1, -1):
        value = jnp.where(i == k, float(table[k]), value)
    return value


def line_apply(v, kappa):
    p = [v[0]] + [v[j] + v[7 - j] for j in range(1, 4)]
    q = [v[0]] + [v[j] - v[7 - j] for j in range(1, 4)]
    a, b = [], []
    for m in range(4):
        even = total(EVEN[m][k] * p[k] for k in range(4))
        odd = total(ODD[m][k] * q[k] for k in range(4))
        first = kappa[m] * (odd + even)
        if 7 - m < len(kappa):
            last = kappa[7 - m] * (odd - even)
            a.append(first - last)
            b.append(first + last)
        else:
            a.append(first)
            b.append(first)
    out = [None] * 8
    for k in range(4):
        r = total(EVEN[m][k] * a[m] for m in range(4))
        t = total(ODD[m][k] * b[m] for m in range(4))
        out[k] = r + t
        if k:
            out[7 - k] = r - t
    return out[:7]


def turned(tile, s):
    return pltpu.roll(tile, 8 - s, 0) if s else tile


def z_apply(closed, diagonals):
    terms = [diagonals[0] * closed, diagonals[4] * turned(closed, 4)]
    for s in range(1, 4):
        terms.append(diagonals[s] * turned(closed, s))
        terms.append(pltpu.roll(diagonals[s] * closed, s, 0))
    return total(terms)


CHIPS = 128
Z_ORDER = (4, 3, 5, 2, 6, 1, 7, 0)
GREETINGS = (("z", 1), ("z", 2), ("x", 1), ("x", 1), ("y", 1), ("y", 1))


def main_kernel(
    f_hbm, x_hbm, fv_hbm, m_hbm, z_hbm,
    v1, v2, v3, coef,
    f7, x7, fv7, m7, zc, v0, fm, cv, closing, acc, kx, ky, bx, by, zd, mdi, dg,
    s_out, rv, rs, rb, row_out, rows_in,
    load_sem, send_sem, recv_sem, set_send, set_recv, row_send, row_recv, greet_sem,
):
    px = lax.axis_index("px")
    py = lax.axis_index("py")
    not_first = py > 0
    not_last = py < 7
    prev_x, next_x = (lax.rem(px + 31, 32), py), (lax.rem(px + 1, 32), py)
    prev_y, next_y = (px, lax.rem(py + 7, 8)), (px, lax.rem(py + 1, 8))

    loads = [
        pltpu.make_async_copy(src, dst, load_sem.at[i])
        for i, (src, dst) in enumerate(
            ((fv_hbm, fv7), (x_hbm, x7), (f_hbm, f7), (z_hbm, zc), (m_hbm, m7))
        )
    ]
    for load in loads:
        load.start()

    at = {"x": px // 8, "y": lax.rem(px // 2, 4), "z": py}
    core = lax.rem(px, 2)
    other_core = (px + 1 - 2 * core, py)

    def chip(x=0, y=0, z=0):
        nx, ny, nz = lax.rem(at["x"] + x, 4), lax.rem(at["y"] + y, 4), lax.rem(at["z"] + z, 8)
        return (nx * 8 + ny * 2 + core, nz)

    def around(axis, distance):
        return chip(**{axis: distance}), chip(**{axis: (8 if axis == "z" else 4) - distance})

    barrier = pltpu.get_barrier_semaphore()
    greeted = (*around("y", 1), *around("x", 1), *around("z", 1), prev_x, next_x)
    for device in greeted:
        pl.semaphore_signal(barrier, inc=1, device_id=device, device_id_type=MESH)

    def greet(step):
        if step:
            pl.semaphore_wait(greet_sem.at[step - 1], 2)
        if step < len(GREETINGS):
            for device in around(*GREETINGS[step]):
                pl.semaphore_signal(
                    greet_sem.at[step], inc=1, device_id=device, device_id_type=MESH
                )

    zero_row = jnp.zeros((1, 128), jnp.float32)
    zero_face = jnp.zeros((7, 8, 128), jnp.float32)

    @pl.when(py == 0)
    def _():
        rb[1] = zero_face
        for r in range(3):
            for c in range(3):
                rs[r, c, 1, 0] = zero_face
                rs[r, c, 1, 1] = zero_face

    @pl.when(py == 7)
    def _():
        ky[:, 7] = zero_face
        for r in range(3):
            for c in range(3):
                rv[r, c, 1] = zero_face

    rows = lax.broadcasted_iota(jnp.int32, (8, 128), 0)
    lanes = lax.broadcasted_iota(jnp.int32, (8, 128), 1)
    last_row = rows == 7
    each = functools.partial(lax.fori_loop, 0, 7)
    whole = functools.partial(lax.fori_loop, 0, 7, unroll=True)

    loads[0].wait()

    def viscosity(x, carry):
        for y in range(7):
            speed = [fv7[i, x, y].astype(jnp.float32) for i in range(3)]
            cv[x, y, 0:7, :] = 0.5 + 0.5 * (
                speed[0] * speed[0] + speed[1] * speed[1] + speed[2] * speed[2]
            )
        return carry

    cv[:, :, 7:8, :] = jnp.zeros((7, 7, 1, 128), jnp.float32)
    whole(viscosity, 0)
    loads[3].wait()
    nwa = zc[NZ * 8 + 1]

    def coefficients(x, carry):
        wx, nwx = by_index(x, QW), by_index(x, NW)
        for y in range(7):
            base = cv[x, y] * nwa
            kx[x, y] = base * (wx * float(NW[y]))
            ky[x, y] = base * (nwx * float(QW[y]))
        return carry

    whole(coefficients, 0)

    def remote(src, dst, send, recv, device):
        return pltpu.make_async_remote_copy(
            src_ref=src,
            dst_ref=dst,
            send_sem=send,
            recv_sem=recv,
            device_id=device,
            device_id_type=MESH,
        )

    setup_copies = [
        remote(kx.at[0], kx.at[7], set_send.at[0], set_recv.at[0], prev_x),
        remote(ky.at[:, 0], ky.at[:, 7], set_send.at[1], set_recv.at[1], prev_y),
        remote(bx.at[7], rb.at[0], set_send.at[2], set_recv.at[2], next_x),
        remote(by.at[:, 7], rb.at[1], set_send.at[3], set_recv.at[3], next_y),
    ]
    vecs = (v0, v1, v2, v3)

    def face_copies(r, c):
        extra = 2 if r == 0 else 1
        v = vecs[r]
        ends = (
            (v.at[c, 0], rv.at[r, c, 0], prev_x),
            (v.at[c, :, 0], rv.at[r, c, 1], prev_y),
            (s_out.at[r, c, 0, 0:extra], rs.at[r, c, 0, 0:extra], next_x),
            (s_out.at[r, c, 1, 0:extra], rs.at[r, c, 1, 0:extra], next_y),
        )
        return [
            remote(src, dst, send_sem.at[r, c, i], recv_sem.at[r, c, i], device)
            for i, (src, dst, device) in enumerate(ends)
        ]

    def start(copies):
        copies[0].start()
        pl.when(not_first)(copies[1].start)
        copies[2].start()
        pl.when(not_last)(copies[3].start)

    def wait_recv(copies):
        copies[0].wait_recv()
        pl.when(not_last)(copies[1].wait_recv)
        copies[2].wait_recv()
        pl.when(not_first)(copies[3].wait_recv)

    def wait_send(copies):
        copies[0].wait_send()
        pl.when(not_first)(copies[1].wait_send)
        copies[2].wait_send()
        pl.when(not_last)(copies[3].wait_send)

    def last_rows(i, carry):
        along_x = [kx[m, i] for m in range(7)]
        for k in range(8):
            bx[k, i] = total(float(DM[m, k] * DM[m, 7]) * along_x[m] for m in range(7))
        along_y = [ky[i, m] for m in range(7)]
        for k in range(8):
            by[i, k] = total(float(DM[m, k] * DM[m, 7]) * along_y[m] for m in range(7))
        return carry

    whole(last_rows, 0)

    loads[1].wait()

    def spread_guess(x, carry):
        for c in range(3):
            for y in range(7):
                v0[c, x, y, 0:7, :] = x7[c, x, y]
                v0[c, x, y, 7:8, :] = zero_row
        return carry

    whole(spread_guess, 0)

    for c in range(3):

        def first_sums(i, carry, c=c):
            v = [v0[c, k, i] for k in range(7)]
            s_out[0, c, 0, 0, i] = total(bx[k, i] * v[k] for k in range(7))
            s_out[0, c, 0, 1, i] = total(float(DM[7, k]) * v[k] for k in range(7))
            v = [v0[c, i, k] for k in range(7)]
            s_out[0, c, 1, 0, i] = total(by[i, k] * v[k] for k in range(7))
            s_out[0, c, 1, 1, i] = total(float(DM[7, k]) * v[k] for k in range(7))
            return carry

        whole(first_sums, 0)

    pl.semaphore_wait(barrier, len(greeted))
    greet(0)
    setup_copies[0].start()
    pl.when(not_first)(setup_copies[1].start)
    setup_copies[2].start()
    pl.when(not_last)(setup_copies[3].start)
    for c in range(3):
        start(face_copies(0, c))

    loads[2].wait()

    def spread_forcing(x, carry):
        nwx = by_index(x, NW)
        for c in range(3):
            for y in range(7):
                fm[c, x, y, 0:7, :] = f7[c, x, y] * (nwa[0:7] * (nwx * float(NW[y])))
                fm[c, x, y, 7:8, :] = zero_row
        return carry

    each(spread_forcing, 0)

    wz = zc[NZ * 8]

    for x in range(7):
        cv[x, :, 7, :] = pltpu.roll(cv[x, :, 0, :], 127, 1)

    def z_setup(x, carry):
        nwx = by_index(x, NW)
        for y in range(7):
            kz = cv[x, y] * (wz * (nwx * float(NW[y])))
            turns = [turned(kz, t) for t in range(8)]
            for s in range(NZ):
                value = total(zc[s * 8 + t] * turns[t] for t in range(8))
                if s == 0:
                    value = value + nwa * (nwx * float(HELMHOLTZ * NW[y]))
                zd[x, y, s] = value
        return carry

    each(z_setup, 0)
    greet(1)

    def local_apply(r):
        v_ref = vecs[r]
        points = 8 if r else 7
        for c in range(3):
            for x in range(7):
                closing[c, x] = pltpu.roll(v_ref[c, x, :, 0, :], 127, 1)
        for c in range(3):

            def x_lines(y, carry, c=c):
                out = line_apply(
                    [v_ref[c, k, y] for k in range(7)], [kx[m, y] for m in range(points)]
                )
                for k in range(7):
                    acc[c, k, y] = out[k]
                return carry

            each(x_lines, 0)

            def yz_lines(x, carry, c=c):
                v = [v_ref[c, x, k] for k in range(7)]
                out = line_apply(v, [ky[x, m] for m in range(points)])
                for k in range(7):
                    closed = jnp.where(last_row, closing[c, x, k : k + 1, :], v[k])
                    z_part = z_apply(closed, [zd[x, k, s] for s in range(NZ)])
                    acc[c, x, k] = acc[c, x, k] + out[k] + z_part
                return carry

            each(yz_lines, 0)
        for c in range(3):
            for x in range(7):
                acc[c, x, :, 0, :] = acc[c, x, :, 0, :] + pltpu.roll(acc[c, x, :, 7, :], 1, 1)

    local_apply(0)
    greet(2)

    loads[4].wait()
    setup_copies[0].wait_recv()
    pl.when(not_last)(setup_copies[1].wait_recv)
    setup_copies[2].wait_recv()
    pl.when(not_first)(setup_copies[3].wait_recv)
    setup_copies[2].wait_send()
    pl.when(not_last)(setup_copies[3].wait_send)
    inner_y = jnp.where(not_first, D77 * D77, 0.0)

    def first_layers(i, carry):
        layer_x = rb[0, i] + (D77 * D77) * kx[0, i]
        layer_y = rb[1, i] + inner_y * ky[i, 0]
        zd[0, i, 0] = zd[0, i, 0] + layer_x
        zd[i, 0, 0] = zd[i, 0, 0] + layer_y
        for c in range(3):
            acc[c, 0, i] = acc[c, 0, i] + layer_x * v0[c, 0, i]
            acc[c, i, 0] = acc[c, i, 0] + layer_y * v0[c, i, 0]
        return carry

    each(first_layers, 0)

    def x_diagonal(y, carry):
        kappa = [kx[m, y] for m in range(8)]
        for k in range(7):
            dg[k, y] = total(float(DM[m, k] ** 2) * kappa[m] for m in range(8))
            bx[k, y] = bx[k, y] + float(DM[7, k] * D77) * kappa[7]
        return carry

    each(x_diagonal, 0)

    for x in range(7):
        dg[x, :, 0, :] = dg[x, :, 0, :] + pltpu.roll(zd[x, :, 0, 7, :], 1, 1)

    def y_diagonal(x, carry):
        kappa = [ky[x, m] for m in range(8)]
        for k in range(7):
            value = total(float(DM[m, k] ** 2) * kappa[m] for m in range(8))
            by[x, k] = by[x, k] + float(DM[7, k] * D77) * kappa[7]
            value = value + dg[x, k] + zd[x, k, 0]
            dg[x, k] = jnp.where(last_row, 0.0, value)
            mdi[x, k, 0:7, :] = m7[x, k].astype(jnp.float32) / value[0:7]
            mdi[x, k, 7:8, :] = zero_row
        return carry

    each(y_diagonal, 0)
    greet(3)

    zero_tile = jnp.zeros((8, 128), jnp.float32)
    moments = {}

    def finish(r, c):
        v_ref, u_ref = vecs[r], vecs[r + 1]
        for i in range(7):
            sum_x, sum_y = rs[r, c, 0, 0, i], rs[r, c, 1, 0, i]
            if r == 0:
                sum_x = sum_x + D77 * kx[0, i] * rs[r, c, 0, 1, i]
                sum_y = sum_y + D77 * ky[i, 0] * rs[r, c, 1, 1, i]
            acc[c, 0, i] = acc[c, 0, i] + sum_x
            acc[c, i, 0] = acc[c, i, 0] + sum_y

        def row(x, carry):
            sums, tally = carry
            sums, tally = list(sums), list(tally)
            end_y = rv[r, c, 1, x]
            sum_y = []
            if r == 0:
                at_end = by_table(x, DM[7])
                last_y = ky[x, 7] * s_out[0, c, 1, 1, x]
            for y in range(7):
                b_x, b_y = bx[x, y], by[x, y]
                t = acc[c, x, y] + b_x * rv[r, c, 0, y] + b_y * end_y
                if r == 0:
                    t = t + at_end * (kx[7, y] * s_out[0, c, 0, 1, y]) + float(DM[7, y]) * last_y
                    u = mdi[x, y] * (fm[c, x, y] - t)
                else:
                    v = v_ref[c, x, y]
                    u = v - mdi[x, y] * t
                u_ref[c, x, y] = u
                if r < 2:
                    sums[y] = sums[y] + b_x * u
                    sum_y.append(b_y * u)
                weighted = dg[x, y] * u
                if r:
                    tally[0] = tally[0] + v * weighted
                tally[1] = tally[1] + u * weighted
            if r < 2:
                s_out[r + 1, c, 1, 0, x] = total(sum_y)
            return tuple(sums), tuple(tally)

        sums, tally = whole(row, ((zero_tile,) * (7 if r < 2 else 0), (zero_tile,) * 2))
        if r < 2:
            for y in range(7):
                s_out[r + 1, c, 0, 0, y] = sums[y]
        if r:
            moments[2 * r - 1, c] = tally[0]
        moments[2 * r, c] = tally[1]

    for r in range(3):
        if r:
            local_apply(r)
            if r == 1:
                greet(5)
        for c in range(3):
            wait_recv(face_copies(r, c))
            finish(r, c)
            if r < 2:
                start(face_copies(r + 1, c))
        if r == 0:
            greet(4)
        if r == 1:
            greet(6)

    halves = []
    for half in range(2):
        stack = zero_tile
        for j in range(8):
            index = half * 8 + j
            if index < 15:
                value = jnp.sum(moments[index // 3, index % 3], axis=0, keepdims=True)
                stack = jnp.where(rows == j, value, stack)
        value = jnp.sum(stack, axis=1, keepdims=True)
        halves.append(jnp.where(lanes == rows + 8 * half, value, 0.0))
    row_total = jnp.sum(halves[0] + halves[1], axis=0, keepdims=True)

    row_out[0] = row_total
    pair = remote(row_out.at[0], rows_in.at[CHIPS - 1], row_send.at[0], row_recv.at[0], other_core)
    pair.start()
    pair.wait_recv()
    row_total = row_total + rows_in[CHIPS - 1]
    row_out[1] = row_total
    for place, dz in enumerate(Z_ORDER):

        def send(i, carry, place=place, dz=dz):
            remote(
                row_out.at[1],
                rows_in.at[16 * place + i],
                row_send.at[1],
                row_recv.at[1],
                chip(3 - i // 4, 3 - lax.rem(i, 4), dz),
            ).start()
            return carry

        lax.fori_loop(0, 16 if dz else 15, send, 0)
    everything = rows_in.at[pl.ds(0, CHIPS - 1)]
    pltpu.make_async_copy(everything, everything, row_recv.at[1]).wait()
    row_total = total([row_total] + [rows_in[slot] for slot in range(CHIPS - 1)])

    n = []
    for k in range(5):
        picked = jnp.where(lanes == rows + 3 * k, jnp.broadcast_to(row_total, (8, 128)), 0.0)
        n.append(jnp.broadcast_to(jnp.sum(picked, axis=1, keepdims=True), (8, 128)))
    alpha0 = n[0] / (n[0] - n[1])
    a = -n[1] / (n[0] - n[1])
    e1 = a * a * n[0] + 2.0 * a * alpha0 * n[1] + alpha0 * alpha0 * n[2]
    b = a + e1 / n[0]
    curvature = (
        b * b * (n[0] - n[1]) + 2.0 * b * alpha0 * (n[1] - n[2]) + alpha0 * alpha0 * (n[2] - n[3])
    )
    alpha1 = e1 / curvature
    a0 = a - alpha1 * b
    a1 = alpha0 - alpha1 * (alpha0 - b)
    a2 = alpha1 * alpha0
    e2 = (
        a0 * a0 * n[0]
        + 2.0 * a0 * a1 * n[1]
        + (a1 * a1 + 2.0 * a0 * a2) * n[2]
        + 2.0 * a1 * a2 * n[3]
        + a2 * a2 * n[4]
    )
    beta1 = e2 / e1
    coef[0] = alpha0 + alpha1 * b
    coef[1] = a2
    coef[2] = a0 + beta1 * b
    coef[3] = a1 + beta1 * alpha0
    coef[4] = a2

    setup_copies[0].wait_send()
    pl.when(not_first)(setup_copies[1].wait_send)
    for r in range(3):
        for c in range(3):
            wait_send(face_copies(r, c))
    pair.wait_send()
    pltpu.make_async_copy(everything, everything, row_send.at[1]).wait()


def body(forcing, initial_guess, forward_velocity, free_mask):
    field = (3, 7, 7, 8, 128)
    plane = (7, 7, 8, 128)
    f32 = jnp.float32
    hbm = pl.BlockSpec(memory_space=pltpu.HBM)
    vmem = pl.BlockSpec(memory_space=pltpu.VMEM)
    v1, v2, v3, coef = pl.pallas_call(
        main_kernel,
        out_shape=[jax.ShapeDtypeStruct(field, f32)] * 3
        + [jax.ShapeDtypeStruct((5, 8, 128), f32)],
        in_specs=[hbm] * 5,
        out_specs=[vmem] * 4,
        scratch_shapes=[
            pltpu.VMEM((3, 7, 7, 7, 128), f32),
            pltpu.VMEM((3, 7, 7, 7, 128), f32),
            pltpu.VMEM((3, 7, 7, 7, 128), jnp.bfloat16),
            pltpu.VMEM((7, 7, 7, 128), jnp.int32),
            pltpu.VMEM((NZ * 8 + 2, 8, 128), f32),
            pltpu.VMEM(field, f32),
            pltpu.VMEM(field, f32),
            pltpu.VMEM(plane, f32),
            pltpu.VMEM((3, 7, 7, 128), f32),
            pltpu.VMEM(field, f32),
            pltpu.VMEM((8, 7, 8, 128), f32),
            pltpu.VMEM((7, 8, 8, 128), f32),
            pltpu.VMEM((8, 7, 8, 128), f32),
            pltpu.VMEM((7, 8, 8, 128), f32),
            pltpu.VMEM((7, 7, NZ, 8, 128), f32),
            pltpu.VMEM(plane, f32),
            pltpu.VMEM(plane, f32),
            pltpu.VMEM((3, 3, 2, 2, 7, 8, 128), f32),
            pltpu.VMEM((3, 3, 2, 7, 8, 128), f32),
            pltpu.VMEM((3, 3, 2, 2, 7, 8, 128), f32),
            pltpu.VMEM((2, 7, 8, 128), f32),
            pltpu.VMEM((2, 1, 128), f32),
            pltpu.VMEM((CHIPS, 1, 128), f32),
            pltpu.SemaphoreType.DMA((5,)),
            pltpu.SemaphoreType.DMA((3, 3, 4)),
            pltpu.SemaphoreType.DMA((3, 3, 4)),
            pltpu.SemaphoreType.DMA((4,)),
            pltpu.SemaphoreType.DMA((4,)),
            pltpu.SemaphoreType.DMA((2,)),
            pltpu.SemaphoreType.DMA((2,)),
            pltpu.SemaphoreType.REGULAR((len(GREETINGS),)),
        ],
        compiler_params=pltpu.CompilerParams(
            collective_id=0, has_side_effects=True, vmem_limit_bytes=32 << 20
        ),
    )(*[pltpu.with_memory_space_constraint(q, pltpu.HBM) for q in (forcing, initial_guess, forward_velocity, free_mask, jnp.asarray(z_constants()))])
    v1, v2, v3 = (v[..., :7, :] for v in (v1, v2, v3))
    coef = coef[:, :3, None, None, None, :]
    guess = initial_guess + coef[0] * v1 + coef[1] * v2
    direction = coef[2] * v1 + coef[3] * v2 + coef[4] * v3
    return guess, direction


def solution(mesh):
    placed = (
        P(None, "px", "py", None, None),
        P(None, "px", "py", None, None),
        P(None, "px", "py", None, None),
        P("px", "py", None, None),
    )
    return jax.shard_map(
        body,
        mesh=mesh,
        in_specs=placed,
        out_specs=(P(None, "px", "py", None, None), P(None, "px", "py", None, None)),
        check_vma=False,
    )
```

```python
import functools

import jax
import jax.numpy as jnp
import numpy as np
from jax import lax
from jax.experimental import pallas as pl
from jax.experimental.pallas import tpu as pltpu
from jax.sharding import PartitionSpec as P

MESH = pl.DeviceIdType.MESH
HELMHOLTZ = 20.0


def gll_tables():
    poly_order = 7
    gll_points = np.array(
        [
            -1.0,
            -0.8717401485096066,
            -0.5917001814331423,
            -0.20929921790247888,
            0.20929921790247888,
            0.5917001814331423,
            0.8717401485096066,
            1.0,
        ]
    )
    previous = np.ones(8)
    legendre = gll_points.copy()
    for degree in range(1, poly_order):
        following = ((2 * degree + 1) * gll_points * legendre - degree * previous) / (degree + 1)
        previous = legendre
        legendre = following
    quad_weights = 2.0 / (poly_order * (poly_order + 1) * legendre**2)
    derivative = np.zeros((8, 8))
    for target in range(8):
        for source in range(8):
            if target != source:
                derivative[target, source] = (
                    legendre[target] / legendre[source] / (gll_points[target] - gll_points[source])
                )
    derivative[0, 0] = -poly_order * (poly_order + 1) / 4.0
    derivative[7, 7] = poly_order * (poly_order + 1) / 4.0
    node_weights = quad_weights[:7].copy()
    node_weights[0] = 2.0 * quad_weights[0]
    return quad_weights, derivative, node_weights


QW, DM, NW = gll_tables()
EVEN = [[float(DM[m, k] + DM[m, 7 - k]) / 2 for k in range(4)] for m in range(4)]
ODD = [[float(DM[m, k] - DM[m, 7 - k]) / 2 for k in range(4)] for m in range(4)]
D77 = float(DM[7, 7])

NZ = 5


def z_constants():
    table = np.zeros((NZ * 8 + 2, 8, 128), np.float32)
    for s in range(NZ):
        for t in range(8):
            for a in range(8):
                m = (a + t) % 8
                table[s * 8 + t, a, :] = DM[m, a] * DM[m, (a + s) % 8]
    for a in range(8):
        table[NZ * 8, a, :] = QW[a]
        table[NZ * 8 + 1, a, :] = NW[a] if a < 7 else 0.0
    return table


def total(terms):
    terms = list(terms)
    while len(terms) > 1:
        terms = [
            terms[i] + terms[i + 1] if i + 1 < len(terms) else terms[i]
            for i in range(0, len(terms), 2)
        ]
    return terms[0]


def by_index(i, table):
    inner = jnp.where((i == 2) | (i == 5), float(table[2]), float(table[3]))
    inner = jnp.where((i == 1) | (i == 6), float(table[1]), inner)
    return jnp.where(i == 0, float(table[0]), inner)


def by_table(i, table):
    value = float(table[6])
    for k in range(5, -1, -1):
        value = jnp.where(i == k, float(table[k]), value)
    return value


def line_apply(v, kappa):
    p = [v[0]] + [v[j] + v[7 - j] for j in range(1, 4)]
    q = [v[0]] + [v[j] - v[7 - j] for j in range(1, 4)]
    a, b = [], []
    for m in range(4):
        even = total(EVEN[m][k] * p[k] for k in range(4))
        odd = total(ODD[m][k] * q[k] for k in range(4))
        first = kappa[m] * (odd + even)
        if 7 - m < len(kappa):
            last = kappa[7 - m] * (odd - even)
            a.append(first - last)
            b.append(first + last)
        else:
            a.append(first)
            b.append(first)
    out = [None] * 8
    for k in range(4):
        r = total(EVEN[m][k] * a[m] for m in range(4))
        t = total(ODD[m][k] * b[m] for m in range(4))
        out[k] = r + t
        if k:
            out[7 - k] = r - t
    return out[:7]


def turned(tile, s):
    return pltpu.roll(tile, 8 - s, 0) if s else tile


def z_apply(closed, diagonals):
    terms = [diagonals[0] * closed, diagonals[4] * turned(closed, 4)]
    for s in range(1, 4):
        terms.append(diagonals[s] * turned(closed, s))
        terms.append(pltpu.roll(diagonals[s] * closed, s, 0))
    return total(terms)


CHIPS = 128
Z_ORDER = (4, 3, 5, 2, 6, 1, 7, 0)
GREETINGS = (("z", 1), ("z", 2), ("x", 1), ("x", 1), ("y", 1), ("y", 1))


def main_kernel(
    f_hbm, x_hbm, fv_hbm, m_hbm, z_hbm,
    v1, v2, v3, coef,
    f7, x7, fv7, m7, zc, v0, fm, cv, closing, acc, kx, ky, bx, by, zd, mdi, dg,
    s_out, rv, rs, rb, row_out, rows_in,
    load_sem, send_sem, recv_sem, set_send, set_recv, row_send, row_recv, greet_sem,
):
    px = lax.axis_index("px")
    py = lax.axis_index("py")
    not_first = py > 0
    not_last = py < 7
    prev_x, next_x = (lax.rem(px + 31, 32), py), (lax.rem(px + 1, 32), py)
    prev_y, next_y = (px, lax.rem(py + 7, 8)), (px, lax.rem(py + 1, 8))

    loads = [
        pltpu.make_async_copy(src, dst, load_sem.at[i])
        for i, (src, dst) in enumerate(
            ((fv_hbm, fv7), (x_hbm, x7), (f_hbm, f7), (z_hbm, zc), (m_hbm, m7))
        )
    ]
    for load in loads:
        load.start()

    at = {"x": px // 8, "y": lax.rem(px // 2, 4), "z": py}
    core = lax.rem(px, 2)
    other_core = (px + 1 - 2 * core, py)

    def chip(x=0, y=0, z=0):
        nx, ny, nz = lax.rem(at["x"] + x, 4), lax.rem(at["y"] + y, 4), lax.rem(at["z"] + z, 8)
        return (nx * 8 + ny * 2 + core, nz)

    def around(axis, distance):
        return chip(**{axis: distance}), chip(**{axis: (8 if axis == "z" else 4) - distance})

    barrier = pltpu.get_barrier_semaphore()
    greeted = (*around("y", 1), *around("x", 1), *around("z", 1), prev_x, next_x)
    for device in greeted:
        pl.semaphore_signal(barrier, inc=1, device_id=device, device_id_type=MESH)

    def greet(step):
        if step:
            pl.semaphore_wait(greet_sem.at[step - 1], 2)
        if step < len(GREETINGS):
            for device in around(*GREETINGS[step]):
                pl.semaphore_signal(
                    greet_sem.at[step], inc=1, device_id=device, device_id_type=MESH
                )

    zero_row = jnp.zeros((1, 128), jnp.float32)
    zero_face = jnp.zeros((7, 8, 128), jnp.float32)

    @pl.when(py == 0)
    def _():
        rb[1] = zero_face
        for r in range(3):
            for c in range(3):
                rs[r, c, 1, 0] = zero_face
                rs[r, c, 1, 1] = zero_face

    @pl.when(py == 7)
    def _():
        ky[:, 7] = zero_face
        for r in range(3):
            for c in range(3):
                rv[r, c, 1] = zero_face

    rows = lax.broadcasted_iota(jnp.int32, (8, 128), 0)
    lanes = lax.broadcasted_iota(jnp.int32, (8, 128), 1)
    last_row = rows == 7
    each = functools.partial(lax.fori_loop, 0, 7)
    whole = functools.partial(lax.fori_loop, 0, 7, unroll=True)

    loads[0].wait()

    def viscosity(x, carry):
        for y in range(7):
            speed = [fv7[i, x, y].astype(jnp.float32) for i in range(3)]
            cv[x, y, 0:7, :] = 0.5 + 0.5 * (
                speed[0] * speed[0] + speed[1] * speed[1] + speed[2] * speed[2]
            )
        return carry

    cv[:, :, 7:8, :] = jnp.zeros((7, 7, 1, 128), jnp.float32)
    whole(viscosity, 0)
    loads[3].wait()
    nwa = zc[NZ * 8 + 1]

    def coefficients(x, carry):
        wx, nwx = by_index(x, QW), by_index(x, NW)
        for y in range(7):
            base = cv[x, y] * nwa
            kx[x, y] = base * (wx * float(NW[y]))
            ky[x, y] = base * (nwx * float(QW[y]))
        return carry

    whole(coefficients, 0)

    def remote(src, dst, send, recv, device):
        return pltpu.make_async_remote_copy(
            src_ref=src,
            dst_ref=dst,
            send_sem=send,
            recv_sem=recv,
            device_id=device,
            device_id_type=MESH,
        )

    setup_copies = [
        remote(kx.at[0], kx.at[7], set_send.at[0], set_recv.at[0], prev_x),
        remote(ky.at[:, 0], ky.at[:, 7], set_send.at[1], set_recv.at[1], prev_y),
        remote(bx.at[7], rb.at[0], set_send.at[2], set_recv.at[2], next_x),
        remote(by.at[:, 7], rb.at[1], set_send.at[3], set_recv.at[3], next_y),
    ]
    vecs = (v0, v1, v2, v3)

    def face_copies(r, c):
        extra = 2 if r == 0 else 1
        v = vecs[r]
        ends = (
            (v.at[c, 0], rv.at[r, c, 0], prev_x),
            (v.at[c, :, 0], rv.at[r, c, 1], prev_y),
            (s_out.at[r, c, 0, 0:extra], rs.at[r, c, 0, 0:extra], next_x),
            (s_out.at[r, c, 1, 0:extra], rs.at[r, c, 1, 0:extra], next_y),
        )
        return [
            remote(src, dst, send_sem.at[r, c, i], recv_sem.at[r, c, i], device)
            for i, (src, dst, device) in enumerate(ends)
        ]

    def start(copies):
        pl.when(not_last)(copies[3].start)
        copies[2].start()
        pl.when(not_first)(copies[1].start)
        copies[0].start()

    def wait_recv(copies):
        copies[0].wait_recv()
        pl.when(not_last)(copies[1].wait_recv)
        copies[2].wait_recv()
        pl.when(not_first)(copies[3].wait_recv)

    def wait_send(copies):
        copies[0].wait_send()
        pl.when(not_first)(copies[1].wait_send)
        copies[2].wait_send()
        pl.when(not_last)(copies[3].wait_send)

    def last_rows(i, carry):
        along_x = [kx[m, i] for m in range(7)]
        for k in range(8):
            bx[k, i] = total(float(DM[m, k] * DM[m, 7]) * along_x[m] for m in range(7))
        along_y = [ky[i, m] for m in range(7)]
        for k in range(8):
            by[i, k] = total(float(DM[m, k] * DM[m, 7]) * along_y[m] for m in range(7))
        return carry

    whole(last_rows, 0)

    loads[1].wait()

    def spread_guess(x, carry):
        for c in range(3):
            for y in range(7):
                v0[c, x, y, 0:7, :] = x7[c, x, y]
                v0[c, x, y, 7:8, :] = zero_row
        return carry

    whole(spread_guess, 0)

    for c in range(3):

        def first_sums(i, carry, c=c):
            v = [v0[c, k, i] for k in range(7)]
            s_out[0, c, 0, 0, i] = total(bx[k, i] * v[k] for k in range(7))
            s_out[0, c, 0, 1, i] = total(float(DM[7, k]) * v[k] for k in range(7))
            v = [v0[c, i, k] for k in range(7)]
            s_out[0, c, 1, 0, i] = total(by[i, k] * v[k] for k in range(7))
            s_out[0, c, 1, 1, i] = total(float(DM[7, k]) * v[k] for k in range(7))
            return carry

        whole(first_sums, 0)

    pl.semaphore_wait(barrier, len(greeted))
    greet(0)
    setup_copies[0].start()
    pl.when(not_first)(setup_copies[1].start)
    setup_copies[2].start()
    pl.when(not_last)(setup_copies[3].start)
    for c in range(3):
        start(face_copies(0, c))

    loads[2].wait()

    def spread_forcing(x, carry):
        nwx = by_index(x, NW)
        for c in range(3):
            for y in range(7):
                fm[c, x, y, 0:7, :] = f7[c, x, y] * (nwa[0:7] * (nwx * float(NW[y])))
                fm[c, x, y, 7:8, :] = zero_row
        return carry

    each(spread_forcing, 0)

    wz = zc[NZ * 8]

    for x in range(7):
        cv[x, :, 7, :] = pltpu.roll(cv[x, :, 0, :], 127, 1)

    def z_setup(x, carry):
        nwx = by_index(x, NW)
        for y in range(7):
            kz = cv[x, y] * (wz * (nwx * float(NW[y])))
            turns = [turned(kz, t) for t in range(8)]
            for s in range(NZ):
                value = total(zc[s * 8 + t] * turns[t] for t in range(8))
                if s == 0:
                    value = value + nwa * (nwx * float(HELMHOLTZ * NW[y]))
                zd[x, y, s] = value
        return carry

    each(z_setup, 0)
    greet(1)

    def local_apply(r):
        v_ref = vecs[r]
        points = 8 if r else 7
        for c in range(3):
            for x in range(7):
                closing[c, x] = pltpu.roll(v_ref[c, x, :, 0, :], 127, 1)
        for c in range(3):

            def x_lines(y, carry, c=c):
                out = line_apply(
                    [v_ref[c, k, y] for k in range(7)], [kx[m, y] for m in range(points)]
                )
                for k in range(7):
                    acc[c, k, y] = out[k]
                return carry

            each(x_lines, 0)

            def yz_lines(x, carry, c=c):
                v = [v_ref[c, x, k] for k in range(7)]
                out = line_apply(v, [ky[x, m] for m in range(points)])
                for k in range(7):
                    closed = jnp.where(last_row, closing[c, x, k : k + 1, :], v[k])
                    z_part = z_apply(closed, [zd[x, k, s] for s in range(NZ)])
                    acc[c, x, k] = acc[c, x, k] + out[k] + z_part
                return carry

            each(yz_lines, 0)
        for c in range(3):
            for x in range(7):
                acc[c, x, :, 0, :] = acc[c, x, :, 0, :] + pltpu.roll(acc[c, x, :, 7, :], 1, 1)

    local_apply(0)
    greet(2)

    loads[4].wait()
    setup_copies[0].wait_recv()
    pl.when(not_last)(setup_copies[1].wait_recv)
    setup_copies[2].wait_recv()
    pl.when(not_first)(setup_copies[3].wait_recv)
    setup_copies[2].wait_send()
    pl.when(not_last)(setup_copies[3].wait_send)
    inner_y = jnp.where(not_first, D77 * D77, 0.0)

    def first_layers(i, carry):
        layer_x = rb[0, i] + (D77 * D77) * kx[0, i]
        layer_y = rb[1, i] + inner_y * ky[i, 0]
        zd[0, i, 0] = zd[0, i, 0] + layer_x
        zd[i, 0, 0] = zd[i, 0, 0] + layer_y
        for c in range(3):
            acc[c, 0, i] = acc[c, 0, i] + layer_x * v0[c, 0, i]
            acc[c, i, 0] = acc[c, i, 0] + layer_y * v0[c, i, 0]
        return carry

    each(first_layers, 0)

    def x_diagonal(y, carry):
        kappa = [kx[m, y] for m in range(8)]
        for k in range(7):
            dg[k, y] = total(float(DM[m, k] ** 2) * kappa[m] for m in range(8))
            bx[k, y] = bx[k, y] + float(DM[7, k] * D77) * kappa[7]
        return carry

    each(x_diagonal, 0)

    for x in range(7):
        dg[x, :, 0, :] = dg[x, :, 0, :] + pltpu.roll(zd[x, :, 0, 7, :], 1, 1)

    def y_diagonal(x, carry):
        kappa = [ky[x, m] for m in range(8)]
        for k in range(7):
            value = total(float(DM[m, k] ** 2) * kappa[m] for m in range(8))
            by[x, k] = by[x, k] + float(DM[7, k] * D77) * kappa[7]
            value = value + dg[x, k] + zd[x, k, 0]
            dg[x, k] = jnp.where(last_row, 0.0, value)
            mdi[x, k, 0:7, :] = m7[x, k].astype(jnp.float32) / value[0:7]
            mdi[x, k, 7:8, :] = zero_row
        return carry

    each(y_diagonal, 0)
    greet(3)

    zero_tile = jnp.zeros((8, 128), jnp.float32)
    moments = {}

    def finish(r, c):
        v_ref, u_ref = vecs[r], vecs[r + 1]
        for i in range(7):
            sum_x, sum_y = rs[r, c, 0, 0, i], rs[r, c, 1, 0, i]
            if r == 0:
                sum_x = sum_x + D77 * kx[0, i] * rs[r, c, 0, 1, i]
                sum_y = sum_y + D77 * ky[i, 0] * rs[r, c, 1, 1, i]
            acc[c, 0, i] = acc[c, 0, i] + sum_x
            acc[c, i, 0] = acc[c, i, 0] + sum_y

        def row(x, carry):
            sums, tally = carry
            sums, tally = list(sums), list(tally)
            end_y = rv[r, c, 1, x]
            sum_y = []
            if r == 0:
                at_end = by_table(x, DM[7])
                last_y = ky[x, 7] * s_out[0, c, 1, 1, x]
            for y in range(7):
                b_x, b_y = bx[x, y], by[x, y]
                t = acc[c, x, y] + b_x * rv[r, c, 0, y] + b_y * end_y
                if r == 0:
                    t = t + at_end * (kx[7, y] * s_out[0, c, 0, 1, y]) + float(DM[7, y]) * last_y
                    u = mdi[x, y] * (fm[c, x, y] - t)
                else:
                    v = v_ref[c, x, y]
                    u = v - mdi[x, y] * t
                u_ref[c, x, y] = u
                if r < 2:
                    sums[y] = sums[y] + b_x * u
                    sum_y.append(b_y * u)
                weighted = dg[x, y] * u
                if r:
                    tally[0] = tally[0] + v * weighted
                tally[1] = tally[1] + u * weighted
            if r < 2:
                s_out[r + 1, c, 1, 0, x] = total(sum_y)
            return tuple(sums), tuple(tally)

        sums, tally = whole(row, ((zero_tile,) * (7 if r < 2 else 0), (zero_tile,) * 2))
        if r < 2:
            for y in range(7):
                s_out[r + 1, c, 0, 0, y] = sums[y]
        if r:
            moments[2 * r - 1, c] = tally[0]
        moments[2 * r, c] = tally[1]

    for r in range(3):
        if r:
            local_apply(r)
            if r == 1:
                greet(5)
        for c in range(3):
            wait_recv(face_copies(r, c))
            finish(r, c)
            if r < 2:
                start(face_copies(r + 1, c))
        if r == 0:
            greet(4)
        if r == 1:
            greet(6)

    halves = []
    for half in range(2):
        stack = zero_tile
        for j in range(8):
            index = half * 8 + j
            if index < 15:
                value = jnp.sum(moments[index // 3, index % 3], axis=0, keepdims=True)
                stack = jnp.where(rows == j, value, stack)
        value = jnp.sum(stack, axis=1, keepdims=True)
        halves.append(jnp.where(lanes == rows + 8 * half, value, 0.0))
    row_total = jnp.sum(halves[0] + halves[1], axis=0, keepdims=True)

    row_out[0] = row_total
    pair = remote(row_out.at[0], rows_in.at[CHIPS - 1], row_send.at[0], row_recv.at[0], other_core)
    pair.start()
    pair.wait_recv()
    row_total = row_total + rows_in[CHIPS - 1]
    row_out[1] = row_total
    for place, dz in enumerate(Z_ORDER):

        def send(i, carry, place=place, dz=dz):
            remote(
                row_out.at[1],
                rows_in.at[16 * place + i],
                row_send.at[1],
                row_recv.at[1],
                chip(3 - i // 4, 3 - lax.rem(i, 4), dz),
            ).start()
            return carry

        lax.fori_loop(0, 16 if dz else 15, send, 0, unroll=4 if dz else 5)
    everything = rows_in.at[pl.ds(0, CHIPS - 1)]
    pltpu.make_async_copy(everything, everything, row_recv.at[1]).wait()
    row_total = total([row_total] + [rows_in[slot] for slot in range(CHIPS - 1)])

    n = []
    for k in range(5):
        picked = jnp.where(lanes == rows + 3 * k, jnp.broadcast_to(row_total, (8, 128)), 0.0)
        n.append(jnp.broadcast_to(jnp.sum(picked, axis=1, keepdims=True), (8, 128)))
    alpha0 = n[0] / (n[0] - n[1])
    a = -n[1] / (n[0] - n[1])
    e1 = a * a * n[0] + 2.0 * a * alpha0 * n[1] + alpha0 * alpha0 * n[2]
    b = a + e1 / n[0]
    curvature = (
        b * b * (n[0] - n[1]) + 2.0 * b * alpha0 * (n[1] - n[2]) + alpha0 * alpha0 * (n[2] - n[3])
    )
    alpha1 = e1 / curvature
    a0 = a - alpha1 * b
    a1 = alpha0 - alpha1 * (alpha0 - b)
    a2 = alpha1 * alpha0
    e2 = (
        a0 * a0 * n[0]
        + 2.0 * a0 * a1 * n[1]
        + (a1 * a1 + 2.0 * a0 * a2) * n[2]
        + 2.0 * a1 * a2 * n[3]
        + a2 * a2 * n[4]
    )
    beta1 = e2 / e1
    coef[0] = alpha0 + alpha1 * b
    coef[1] = a2
    coef[2] = a0 + beta1 * b
    coef[3] = a1 + beta1 * alpha0
    coef[4] = a2

    setup_copies[0].wait_send()
    pl.when(not_first)(setup_copies[1].wait_send)
    for r in range(3):
        for c in range(3):
            wait_send(face_copies(r, c))
    pair.wait_send()
    pltpu.make_async_copy(everything, everything, row_send.at[1]).wait()


def body(forcing, initial_guess, forward_velocity, free_mask):
    field = (3, 7, 7, 8, 128)
    plane = (7, 7, 8, 128)
    f32 = jnp.float32
    hbm = pl.BlockSpec(memory_space=pltpu.HBM)
    vmem = pl.BlockSpec(memory_space=pltpu.VMEM)
    v1, v2, v3, coef = pl.pallas_call(
        main_kernel,
        out_shape=[jax.ShapeDtypeStruct(field, f32)] * 3
        + [jax.ShapeDtypeStruct((5, 8, 128), f32)],
        in_specs=[hbm] * 5,
        out_specs=[vmem] * 4,
        scratch_shapes=[
            pltpu.VMEM((3, 7, 7, 7, 128), f32),
            pltpu.VMEM((3, 7, 7, 7, 128), f32),
            pltpu.VMEM((3, 7, 7, 7, 128), jnp.bfloat16),
            pltpu.VMEM((7, 7, 7, 128), jnp.int32),
            pltpu.VMEM((NZ * 8 + 2, 8, 128), f32),
            pltpu.VMEM(field, f32),
            pltpu.VMEM(field, f32),
            pltpu.VMEM(plane, f32),
            pltpu.VMEM((3, 7, 7, 128), f32),
            pltpu.VMEM(field, f32),
            pltpu.VMEM((8, 7, 8, 128), f32),
            pltpu.VMEM((7, 8, 8, 128), f32),
            pltpu.VMEM((8, 7, 8, 128), f32),
            pltpu.VMEM((7, 8, 8, 128), f32),
            pltpu.VMEM((7, 7, NZ, 8, 128), f32),
            pltpu.VMEM(plane, f32),
            pltpu.VMEM(plane, f32),
            pltpu.VMEM((3, 3, 2, 2, 7, 8, 128), f32),
            pltpu.VMEM((3, 3, 2, 7, 8, 128), f32),
            pltpu.VMEM((3, 3, 2, 2, 7, 8, 128), f32),
            pltpu.VMEM((2, 7, 8, 128), f32),
            pltpu.VMEM((2, 1, 128), f32),
            pltpu.VMEM((CHIPS, 1, 128), f32),
            pltpu.SemaphoreType.DMA((5,)),
            pltpu.SemaphoreType.DMA((3, 3, 4)),
            pltpu.SemaphoreType.DMA((3, 3, 4)),
            pltpu.SemaphoreType.DMA((4,)),
            pltpu.SemaphoreType.DMA((4,)),
            pltpu.SemaphoreType.DMA((2,)),
            pltpu.SemaphoreType.DMA((2,)),
            pltpu.SemaphoreType.REGULAR((len(GREETINGS),)),
        ],
        compiler_params=pltpu.CompilerParams(
            collective_id=0, has_side_effects=True, vmem_limit_bytes=32 << 20
        ),
    )(*[pltpu.with_memory_space_constraint(q, pltpu.HBM) for q in (forcing, initial_guess, forward_velocity, free_mask, jnp.asarray(z_constants()))])
    v1, v2, v3 = (v[..., :7, :] for v in (v1, v2, v3))
    coef = coef[:, :3, None, None, None, :]
    guess = initial_guess + coef[0] * v1 + coef[1] * v2
    direction = coef[2] * v1 + coef[3] * v2 + coef[4] * v3
    return guess, direction


def solution(mesh):
    placed = (
        P(None, "px", "py", None, None),
        P(None, "px", "py", None, None),
        P(None, "px", "py", None, None),
        P("px", "py", None, None),
    )
    return jax.shard_map(
        body,
        mesh=mesh,
        in_specs=placed,
        out_specs=(P(None, "px", "py", None, None), P(None, "px", "py", None, None)),
        check_vma=False,
    )
```
